512 devices in a mesh: row: 16 (over y, core), col: 32 (over x, z).
Axes of the slice: x: 4, y: 8, z: 8, core: 2. Of those that a mesh axis runs over, the one named last changes fastest.
Arguments:
- image_embeddings: float32 [16384, 512], P('row', 'col'), as said below
- text_embeddings: float32 [16384, 512], P('col', 'row'), as said below
- negatives_mask: int32 [64, 64], replicated, may hold values from 0 to 1, as said below
Outputs:
- grad_image: float32 [16384, 512], P('row', 'col')
- grad_text: float32 [16384, 512], P('col', 'row')
The draws below stay inside these ranges and needn't reach their ends.
Inputs may be any that keep to these rules, and one draw needn't show every extreme that they name: `image_embeddings`: embedding entries lie within -4 to 4. `text_embeddings`: embedding entries lie within -4 to 4. `negatives_mask`: 0 or 1; the diagonal blocks are allowed whatever it holds there.
All inputs are finite; a program needn't handle non-finite values.
Results may differ from the reference program's by a relative error of at most 0.0003.
Values sent between devices are 32-bit elements; how exact they have to be, the bound alone decides.
No kernel may reach another device: no remote copies, remote signals or barrier semaphores. Data moves between devices by JAX's collectives and lax.ppermute only.
A program may use at most 64 MiB of HBM per device.

```python
import jax
import jax.numpy as jnp
from jax import lax

D = 512
BLK = 256
PAIRS = 16384
NB = 64


def draw_image_embeddings(key, part):
    key = jax.random.fold_in(key, 11)
    return jnp.clip(jax.random.normal(key, (PAIRS, D), jnp.float32), -4.0, 4.0)


def draw_text_embeddings(key, part):
    key = jax.random.fold_in(key, 23)
    return jnp.clip(jax.random.normal(key, (PAIRS, D), jnp.float32), -4.0, 4.0)


def draw_negatives_mask(key, part):
    key = jax.random.fold_in(key, 5)
    key_level, key_roll = jax.random.split(key)
    level = jax.random.randint(key_level, (NB, 1), 1, 8)
    roll = jax.random.randint(key_roll, (NB, NB), 0, 8)
    return (roll < level).astype(jnp.int32)


def setup_inputs(seed: int = 0) -> dict:
    key_of = jax.random.split(jax.random.key(seed), 4)
    return {
        "image_embeddings": draw_image_embeddings(jax.random.fold_in(key_of[3], 71), 0),
        "text_embeddings": draw_text_embeddings(jax.random.fold_in(key_of[3], 71), 0),
        "negatives_mask": draw_negatives_mask(jax.random.fold_in(key_of[3], 71), 0),
    }


NEG = -1.0e30


def reference(image_embeddings, text_embeddings, negatives_mask):
    inv = D ** -0.5
    col_block = jnp.arange(PAIRS, dtype=jnp.int32) // BLK
    img_blocks = image_embeddings.reshape(NB, BLK, D)
    block_ids = jnp.arange(NB, dtype=jnp.int32)
    cols = jnp.arange(PAIRS, dtype=jnp.int32)

    def allowed_of(bidx):
        row = jnp.repeat(negatives_mask[bidx] > 0, BLK, total_repeat_length=PAIRS)
        allow = row | (col_block == bidx)
        return jnp.broadcast_to(allow[None, :], (BLK, PAIRS))

    def scores(block):
        return jnp.dot(block, text_embeddings.T, precision=lax.Precision.HIGHEST, preferred_element_type=jnp.float32) * inv

    def first_pass(carry, item):
        col_max, col_sum = carry
        block, bidx = item
        logits = scores(block)
        allowed = allowed_of(bidx)
        masked = jnp.where(allowed, logits, NEG)
        row_max = jnp.max(masked, axis=1)
        row_sum = jnp.sum(jnp.where(allowed, jnp.exp(logits - row_max[:, None]), 0.0), axis=1)
        new_max = jnp.maximum(col_max, jnp.max(masked, axis=0))
        new_sum = col_sum * jnp.exp(col_max - new_max) + jnp.sum(jnp.where(allowed, jnp.exp(logits - new_max[None, :]), 0.0), axis=0)
        return (new_max, new_sum), row_max + jnp.log(row_sum)

    init = (jnp.full((PAIRS,), NEG, jnp.float32), jnp.zeros((PAIRS,), jnp.float32))
    (col_max, col_sum), row_lse = lax.scan(first_pass, init, (img_blocks, block_ids))
    col_lse = col_max + jnp.log(col_sum)

    def second_pass(grad_text, item):
        block, bidx, lse = item
        logits = scores(block)
        allowed = allowed_of(bidx)
        eye = ((bidx * BLK + jnp.arange(BLK, dtype=jnp.int32))[:, None] == cols[None, :]).astype(jnp.float32)
        grad_logits = jnp.where(allowed, 0.5 * (jnp.exp(logits - lse[:, None]) + jnp.exp(logits - col_lse[None, :])), 0.0) - eye
        grad_img = jnp.dot(grad_logits, text_embeddings, precision=lax.Precision.HIGHEST, preferred_element_type=jnp.float32) * inv
        grad_text = grad_text + jnp.dot(grad_logits.T, block, precision=lax.Precision.HIGHEST, preferred_element_type=jnp.float32) * inv
        return grad_text, grad_img

    grad_text, grad_img = lax.scan(second_pass, jnp.zeros((PAIRS, D), jnp.float32), (img_blocks, block_ids, row_lse))
    return grad_img.reshape(PAIRS, D), grad_text
```

```python
import jax
import jax.numpy as jnp
from jax import lax
from jax.sharding import Mesh
from jax.sharding import PartitionSpec as P

BLK = 256
NEG = -1e30
ROW = ("y", "core")
COL = ("x", "z")


def gather(block, axis, n):
    copies = jnp.broadcast_to(block[None], (n,) + block.shape)
    got = lax.all_to_all(copies, axis, 0, 0)
    return got.reshape((n * block.shape[0],) + block.shape[1:])


def scatter_sum(terms, axis, n):
    parts = terms.reshape((n, terms.shape[0] // n) + terms.shape[1:])
    return jnp.sum(lax.all_to_all(parts, axis, 0, 0), axis=0)


def total_lse(local, axis, n):
    every = gather(local[None], axis, n)
    top = jnp.max(every, axis=0)
    return top + jnp.log(jnp.sum(jnp.exp(every - top[None]), axis=0))


def body(image_embeddings, text_embeddings, negatives_mask):
    ny, nc, nx, nz = (lax.axis_size(a) for a in ("y", "core", "x", "z"))
    texts = lax.all_gather(text_embeddings.T, ROW, axis=0, tiled=True)
    images = gather(gather(image_embeddings.T, "z", nz), "x", nx)
    rows = images.shape[1]
    cols = texts.shape[1]
    inv = images.shape[0] ** (-0.5)
    row_start = lax.axis_index(ROW) * rows
    col_start = lax.axis_index(COL) * cols
    logits = (
        lax.dot_general(
            images,
            texts,
            (((0,), (0,)), ((), ())),
            precision=lax.Precision.HIGHEST,
            preferred_element_type=jnp.float32,
        )
        * inv
    )
    row_blocks = rows // BLK
    col_blocks = cols // BLK
    first_row = row_start // BLK
    first_col = col_start // BLK
    window = lax.dynamic_slice(negatives_mask, (first_row, first_col), (row_blocks, col_blocks))
    row_ids = first_row + jnp.arange(row_blocks, dtype=jnp.int32)
    col_ids = first_col + jnp.arange(col_blocks, dtype=jnp.int32)
    block_allow = (window > 0) | (row_ids[:, None] == col_ids[None, :])
    allowed = jnp.broadcast_to(
        block_allow[:, None, :, None], (row_blocks, BLK, col_blocks, BLK)
    ).reshape(rows, cols)
    masked = jnp.where(allowed, logits, NEG)

    def local_lse(axis):
        top = jnp.max(masked, axis=axis, keepdims=True)
        total = jnp.sum(jnp.where(allowed, jnp.exp(logits - top), 0.0), axis=axis, keepdims=True)
        return jnp.squeeze(top + jnp.log(jnp.maximum(total, 1e-30)), axis)

    row_lse = total_lse(local_lse(1), COL, nx * nz)
    col_lse = total_lse(local_lse(0), ROW, ny * nc)
    diagonal = (
        (row_start + jnp.arange(rows, dtype=jnp.int32))[:, None]
        == (col_start + jnp.arange(cols, dtype=jnp.int32))[None, :]
    ).astype(jnp.float32)
    grad_logits = (
        jnp.where(
            allowed,
            0.5 * (jnp.exp(logits - row_lse[:, None]) + jnp.exp(logits - col_lse[None, :])),
            0.0,
        )
        - diagonal
    )
    text_terms = (
        lax.dot_general(
            images,
            grad_logits,
            (((1,), (0,)), ((), ())),
            precision=lax.Precision.HIGH,
            preferred_element_type=jnp.float32,
        )
        * inv
    )
    grad_text = lax.psum_scatter(text_terms, ROW, scatter_dimension=0, tiled=True)
    image_terms = (
        lax.dot_general(
            texts,
            grad_logits,
            (((1,), (1,)), ((), ())),
            precision=lax.Precision.HIGH,
            preferred_element_type=jnp.float32,
        )
        * inv
    )
    grad_image = scatter_sum(scatter_sum(image_terms, "x", nx), "z", nz)
    return (grad_image.T, grad_text.T)


def solution(mesh):
    rows, cols = mesh.devices.shape
    fine = Mesh(mesh.devices.reshape(rows // 2, 2, 4, cols // 4), ("y", "core", "x", "z"))
    return jax.shard_map(
        body,
        mesh=fine,
        in_specs=(P(ROW, COL), P(COL, ROW), P()),
        out_specs=(P(ROW, COL), P(COL, ROW)),
        check_vma=False,
    )
```

```python
import jax
import jax.numpy as jnp
from jax import lax
from jax.sharding import Mesh
from jax.sharding import PartitionSpec as P

BLK = 256
NEG = -1e30
ROW = ("y", "core")
COL = ("x", "z")


def gather(block, axis, n):
    copies = jnp.broadcast_to(block[None], (n,) + block.shape)
    got = lax.all_to_all(copies, axis, 0, 0)
    return got.reshape((n * block.shape[0],) + block.shape[1:])


def scatter_sum(terms, axis, n):
    parts = terms.reshape((n, terms.shape[0] // n) + terms.shape[1:])
    return jnp.sum(lax.all_to_all(parts, axis, 0, 0), axis=0)


def flip(axis, n, bit):
    return [(i, i ^ bit) for i in range(n)]


def pair_gather(block, axis, n, bit, dim):
    other = lax.ppermute(block, axis, flip(axis, n, bit))
    low = (lax.axis_index(axis) & bit) == 0
    return jnp.stack([jnp.where(low, block, other), jnp.where(low, other, block)], axis=dim)


def pair_sum(terms, axis, n, bit, dim):
    mine = jnp.where((lax.axis_index(axis) & bit) == 0, 0, 1)
    send = lax.dynamic_index_in_dim(terms, 1 - mine, dim, keepdims=False)
    keep = lax.dynamic_index_in_dim(terms, mine, dim, keepdims=False)
    return keep + lax.ppermute(send, axis, flip(axis, n, bit))


def total_lse(local, axis, n):
    every = gather(local[None], axis, n)
    top = jnp.max(every, axis=0)
    return top + jnp.log(jnp.sum(jnp.exp(every - top[None]), axis=0))


def body(image_embeddings, text_embeddings, negatives_mask):
    ny, nc, nx, nz = (lax.axis_size(a) for a in ("y", "core", "x", "z"))
    texts = text_embeddings.T
    bits = [1 << b for b in reversed(range(ny.bit_length() - 1))]
    for dim, bit in enumerate(bits):
        texts = pair_gather(texts, "y", ny, bit, dim)
    texts = pair_gather(texts, "core", nc, 1, len(bits))
    texts = texts.reshape(-1, texts.shape[-1])
    images = gather(gather(image_embeddings.T, "z", nz), "x", nx)
    rows = images.shape[1]
    cols = texts.shape[1]
    inv = images.shape[0] ** (-0.5)
    row_start = lax.axis_index(ROW) * rows
    col_start = lax.axis_index(COL) * cols
    logits = (
        lax.dot_general(
            images,
            texts,
            (((0,), (0,)), ((), ())),
            precision=lax.Precision.HIGHEST,
            preferred_element_type=jnp.float32,
        )
        * inv
    )
    row_blocks = rows // BLK
    col_blocks = cols // BLK
    first_row = row_start // BLK
    first_col = col_start // BLK
    window = lax.dynamic_slice(negatives_mask, (first_row, first_col), (row_blocks, col_blocks))
    row_ids = first_row + jnp.arange(row_blocks, dtype=jnp.int32)
    col_ids = first_col + jnp.arange(col_blocks, dtype=jnp.int32)
    block_allow = (window > 0) | (row_ids[:, None] == col_ids[None, :])
    allowed = jnp.broadcast_to(
        block_allow[:, None, :, None], (row_blocks, BLK, col_blocks, BLK)
    ).reshape(rows, cols)
    masked = jnp.where(allowed, logits, NEG)

    def local_lse(axis):
        top = jnp.max(masked, axis=axis, keepdims=True)
        total = jnp.sum(jnp.where(allowed, jnp.exp(logits - top), 0.0), axis=axis, keepdims=True)
        return jnp.squeeze(top + jnp.log(jnp.maximum(total, 1e-30)), axis)

    row_lse = total_lse(local_lse(1), COL, nx * nz)
    col_lse = total_lse(local_lse(0), ROW, ny * nc)
    diagonal = (
        (row_start + jnp.arange(rows, dtype=jnp.int32))[:, None]
        == (col_start + jnp.arange(cols, dtype=jnp.int32))[None, :]
    ).astype(jnp.float32)
    grad_logits = (
        jnp.where(
            allowed,
            0.5 * (jnp.exp(logits - row_lse[:, None]) + jnp.exp(logits - col_lse[None, :])),
            0.0,
        )
        - diagonal
    )
    text_terms = (
        lax.dot_general(
            images,
            grad_logits,
            (((1,), (0,)), ((), ())),
            precision=lax.Precision.HIGH,
            preferred_element_type=jnp.float32,
        )
        * inv
    )
    grad_text = text_terms.reshape((2,) * (len(bits) + 1) + (-1, cols))
    grad_text = pair_sum(grad_text, "core", nc, 1, len(bits))
    for dim, bit in reversed(list(enumerate(bits))):
        grad_text = pair_sum(grad_text, "y", ny, bit, dim)
    image_terms = (
        lax.dot_general(
            texts,
            grad_logits,
            (((1,), (1,)), ((), ())),
            precision=lax.Precision.HIGH,
            preferred_element_type=jnp.float32,
        )
        * inv
    )
    grad_image = scatter_sum(scatter_sum(image_terms, "x", nx), "z", nz)
    return (grad_image.T, grad_text.T)


def solution(mesh):
    rows, cols = mesh.devices.shape
    fine = Mesh(mesh.devices.reshape(rows // 2, 2, 4, cols // 4), ("y", "core", "x", "z"))
    return jax.shard_map(
        body,
        mesh=fine,
        in_specs=(P(ROW, COL), P(COL, ROW), P()),
        out_specs=(P(ROW, COL), P(COL, ROW)),
        check_vma=False,
    )
```

```python
import functools

import jax
import jax.numpy as jnp
from jax import lax
from jax.experimental import pallas as pl
from jax.experimental.pallas import tpu as pltpu
from jax.sharding import Mesh
from jax.sharding import PartitionSpec as P

BLK = 256
LANES = 128
NEG = -1e30
ROW = ("y", "core")
COL = ("x", "z")
VMEM = pl.BlockSpec(memory_space=pltpu.VMEM)
HBM = pl.BlockSpec(memory_space=pltpu.HBM)
SMEM = pl.BlockSpec(memory_space=pltpu.SMEM)
ANY = pl.BlockSpec(memory_space=pl.ANY)
PARAMS = pltpu.CompilerParams(vmem_limit_bytes=40 * 2**20)
NN = (((1,), (0,)), ((), ()))
NT = (((1,), (1,)), ((), ()))


def split(x, terms):
    out = []
    for _ in range(terms):
        out.append(x.astype(jnp.bfloat16))
        x = x - out[-1].astype(jnp.float32)
    return out


def product(a, b, dims, order):
    total = None
    for both in range(order, -1, -1):
        for i in range(both + 1):
            if i < len(a) and both - i < len(b):
                p = lax.dot_general(a[i], b[both - i], dims, preferred_element_type=jnp.float32)
                total = p if total is None else total + p
    return total


def natural(me_ref, near_ref, far_ref, texts_ref):
    n, step, _ = near_ref.shape
    core, y = me_ref[0], me_ref[1]
    for k in range(n):
        for other, ref in enumerate((near_ref, far_ref)):
            at = ((y ^ place_of(k)) * 2 + (core ^ other)) * step
            texts_ref[pl.ds(pl.multiple_of(at, step), step), :] = ref[k]


def place_of(k):
    return (k % 2) * 4 + k // 2


def logits_kernel(
    me_ref, allow_ref, images_ref, near_ref, far_ref, logits_ref, row_ref, col_ref, texts_ref
):
    width, rows = images_ref.shape
    cols = texts_ref.shape[1]
    inv = width ** (-0.5)
    natural(me_ref, near_ref, far_ref, texts_ref)
    texts = split(texts_ref[...].T, 3)
    for i in range(rows // BLK):
        at = pl.ds(i * BLK, BLK)
        part = product(texts, split(images_ref[:, at], 3), NN, 2) * inv
        for j in range(cols // BLK):
            block = jnp.where(allow_ref[i, j] > 0, part[j * BLK : (j + 1) * BLK], NEG)
            logits_ref[pl.ds(j * BLK, BLK), at] = block
        part = logits_ref[:, at]
        top = jnp.max(part, axis=0, keepdims=True)
        lse = top + jnp.log(jnp.sum(jnp.exp(part - top), axis=0, keepdims=True))
        put(row_ref, lse, i * BLK // LANES)
    for j in range(cols // BLK):
        part = logits_ref[pl.ds(j * BLK, BLK), :]
        top = jnp.max(part, axis=1, keepdims=True)
        lse = top + jnp.log(jnp.sum(jnp.exp(part - top), axis=1, keepdims=True))
        lse = jnp.broadcast_to(lse, (BLK, LANES)).T[:1]
        for first in range(j * BLK // LANES, col_ref.shape[1], cols // LANES):
            put(col_ref, lse, first)


def put(ref, values, first):
    for k in range(values.shape[1] // LANES):
        row = values[:, k * LANES : (k + 1) * LANES]
        ref[:, pl.ds(first + k, 1), :] = jnp.broadcast_to(row[None], (ref.shape[0], 1, LANES))


def lse_of(parts):
    top = jnp.max(parts, axis=0)
    return top + jnp.log(jnp.sum(jnp.exp(parts - top[None]), axis=0))


def gradient(me_ref, logits_ref, row_ref, col_ref):
    cols, rows = logits_ref.shape
    row_lse = lse_of(row_ref[...])
    col_lse = lse_of(col_ref[...])
    col_lse = jnp.concatenate(
        [jnp.broadcast_to(col_lse[k : k + 1], (LANES, LANES)).T[:, :1] for k in range(cols // LANES)]
    )
    ahead = me_ref[2] - me_ref[3]
    for i in range(rows // BLK):
        part = logits_ref[:, pl.ds(i * BLK, BLK)]
        first = i * BLK // LANES
        row = jnp.concatenate([row_lse[first + k : first + k + 1] for k in range(BLK // LANES)], axis=1)
        grad = 0.5 * (jnp.exp(part - row) + jnp.exp(part - col_lse))
        text_at = lax.broadcasted_iota(jnp.int32, grad.shape, 0)
        image_at = lax.broadcasted_iota(jnp.int32, grad.shape, 1) + (i * BLK + ahead)
        yield pl.ds(i * BLK, BLK), jnp.where(text_at == image_at, grad - 1.0, grad)


def image_kernel(me_ref, logits_ref, row_ref, col_ref, near_ref, far_ref, terms_ref, texts_ref):
    inv = texts_ref.shape[0] ** (-0.5)
    natural(me_ref, near_ref, far_ref, texts_ref)
    texts = split(texts_ref[...], 2)
    for at, grad in gradient(me_ref, logits_ref, row_ref, col_ref):
        terms_ref[:, at] = product(texts, split(grad, 2), NN, 1) * inv


def text_kernel(me_ref, logits_ref, row_ref, col_ref, images_ref, keep_ref, send_ref, all_ref):
    inv = images_ref.shape[0] ** (-0.5)
    total = None
    for at, grad in gradient(me_ref, logits_ref, row_ref, col_ref):
        p = product(split(images_ref[:, at], 2), split(grad, 2), NT, 1)
        total = p if total is None else total + p
    all_ref[...] = total * inv
    n, step, _ = keep_ref.shape
    core, y = me_ref[0], me_ref[1]
    for k in range(n):
        for other, ref in enumerate((keep_ref, send_ref)):
            at = ((y ^ place_of(k)) * 2 + (core ^ other)) * step
            ref[k] = all_ref[pl.ds(pl.multiple_of(at, step), step), :]


def sum_kernel(parts_in, after_ref, out_ref, parts_ref, sems):
    del after_ref
    loads = [
        pltpu.make_async_copy(parts_in.at[k], parts_ref.at[k], sems.at[k]) for k in range(parts_in.shape[0])
    ]
    for load in loads:
        load.start()
    for load in loads:
        load.wait()
    out_ref[...] = jnp.sum(parts_ref[...], axis=0)


def gather(block, axis, n):
    return lax.all_to_all(jnp.broadcast_to(block[None], (n,) + block.shape), axis, 0, 0)


def after(x, y):
    return x + 0.0 * y.reshape(-1)[0]


def sum_of(parts, after):
    return pl.pallas_call(
        sum_kernel,
        out_shape=jax.ShapeDtypeStruct(parts.shape[1:], parts.dtype),
        in_specs=[ANY, ANY],
        scratch_shapes=[pltpu.VMEM(parts.shape, parts.dtype), pltpu.SemaphoreType.DMA((parts.shape[0],))],
        compiler_params=PARAMS,
        name="sum",
    )(parts, after)


def flip(axis, n, bit):
    return [(i, i ^ bit) for i in range(n)]


def body(image_embeddings, text_embeddings, negatives_mask):
    ny, nc, nx, nz = (lax.axis_size(a) for a in ("y", "core", "x", "z"))
    rows, own = image_embeddings.shape
    cols, own_text = text_embeddings.shape
    texts = text_embeddings.T
    far_half = lax.ppermute(texts, "y", flip("y", ny, 4))
    images = gather(image_embeddings.T, "z", nz).reshape(nz * own, rows)
    texts = after(jnp.stack([texts, far_half]), images)
    images = gather(after(images, far_half), "x", nx).reshape(nx * nz * own, rows)
    near = jnp.concatenate([texts] + [lax.ppermute(texts, "y", flip("y", ny, k)) for k in (1, 2, 3)])
    far = lax.ppermute(near, "core", flip("core", nc, 1))
    width = images.shape[0]
    row_start = lax.axis_index(ROW) * rows
    col_start = lax.axis_index(COL) * cols
    row_blocks, col_blocks = rows // BLK, cols // BLK
    first_row, first_col = row_start // BLK, col_start // BLK
    window = lax.dynamic_slice(negatives_mask, (first_row, first_col), (row_blocks, col_blocks))
    row_ids = first_row + jnp.arange(row_blocks, dtype=jnp.int32)
    col_ids = first_col + jnp.arange(col_blocks, dtype=jnp.int32)
    allow = ((window > 0) | (row_ids[:, None] == col_ids[None, :])).astype(jnp.int32)
    f32 = jnp.float32
    passes = 2 * rows * cols * width
    me = [lax.axis_index("core"), lax.axis_index("y"), row_start, col_start]
    me = jnp.stack(me).astype(jnp.int32)
    logits, row_parts, col_parts = pl.pallas_call(
        logits_kernel,
        out_shape=(
            jax.ShapeDtypeStruct((cols, rows), f32),
            jax.ShapeDtypeStruct((nx * nz, rows // LANES, LANES), f32),
            jax.ShapeDtypeStruct((ny * nc, rows // LANES, LANES), f32),
        ),
        in_specs=[SMEM, SMEM, VMEM, VMEM, VMEM],
        out_specs=(VMEM, VMEM, VMEM),
        scratch_shapes=[pltpu.VMEM((width, cols), f32)],
        compiler_params=PARAMS,
        cost_estimate=pl.CostEstimate(flops=6 * passes, bytes_accessed=5 << 20, transcendentals=0),
        name="logits",
    )(me, allow, images, near, far)
    col_parts = lax.all_to_all(col_parts, ROW, 0, 0)
    row_parts = lax.all_to_all(row_parts, COL, 0, 0)
    image_terms = pl.pallas_call(
        image_kernel,
        out_shape=jax.ShapeDtypeStruct((width, rows), f32),
        in_specs=[SMEM, VMEM, VMEM, VMEM, VMEM, VMEM],
        out_specs=VMEM,
        scratch_shapes=[pltpu.VMEM((width, cols), f32)],
        compiler_params=PARAMS,
        cost_estimate=pl.CostEstimate(flops=3 * passes, bytes_accessed=5 << 20, transcendentals=0),
        name="image_terms",
    )(me, logits, row_parts, col_parts, near, far)
    half = jax.ShapeDtypeStruct((ny, own_text, cols), f32)
    keep, send = pl.pallas_call(
        text_kernel,
        out_shape=(half, half),
        in_specs=[SMEM, VMEM, VMEM, VMEM, VMEM],
        out_specs=(VMEM, VMEM),
        scratch_shapes=[pltpu.VMEM((width, cols), f32)],
        compiler_params=PARAMS,
        cost_estimate=pl.CostEstimate(flops=3 * passes, bytes_accessed=5 << 20, transcendentals=0),
        name="text_terms",
    )(me, logits, row_parts, col_parts, images)
    parts = lax.all_to_all(image_terms.reshape(nx, nz * own, rows), "x", 0, 0)
    grad_text = keep + lax.ppermute(send, "core", flip("core", nc, 1))
    grad_text = grad_text.reshape(4, 2, own_text, cols)
    grad_text = sum([lax.ppermute(grad_text[k], "y", flip("y", ny, k)) for k in (1, 2, 3)], grad_text[0])
    parts = sum_of(parts, grad_text)
    grad_text = grad_text[0] + lax.ppermute(grad_text[1], "y", flip("y", ny, 4))
    grad_image = jnp.sum(lax.all_to_all(parts.reshape(nz, own, rows), "z", 0, 0), axis=0)
    return (grad_image.T, grad_text.T)


def solution(mesh):
    rows, cols = mesh.devices.shape
    fine = Mesh(mesh.devices.reshape(rows // 2, 2, 4, cols // 4), ("y", "core", "x", "z"))
    return jax.shard_map(
        body,
        mesh=fine,
        in_specs=(P(ROW, COL), P(COL, ROW), P()),
        out_specs=(P(ROW, COL), P(COL, ROW)),
        check_vma=False,
    )
```

```python
import functools

import jax
import jax.numpy as jnp
from jax import lax
from jax.experimental import pallas as pl
from jax.experimental.pallas import tpu as pltpu
from jax.sharding import Mesh
from jax.sharding import PartitionSpec as P

BLK = 256
LANES = 128
NEG = -1e30
ROW = ("y", "core")
COL = ("x", "z")
VMEM = pl.BlockSpec(memory_space=pltpu.VMEM)
HBM = pl.BlockSpec(memory_space=pltpu.HBM)
SMEM = pl.BlockSpec(memory_space=pltpu.SMEM)
ANY = pl.BlockSpec(memory_space=pl.ANY)
PARAMS = pltpu.CompilerParams(vmem_limit_bytes=40 * 2**20)
NN = (((1,), (0,)), ((), ()))
NT = (((1,), (1,)), ((), ()))


def split(x, terms):
    out = []
    for _ in range(terms):
        out.append(x.astype(jnp.bfloat16))
        x = x - out[-1].astype(jnp.float32)
    return out


def product(a, b, dims, order):
    total = None
    for both in range(order, -1, -1):
        for i in range(both + 1):
            if i < len(a) and both - i < len(b):
                p = lax.dot_general(a[i], b[both - i], dims, preferred_element_type=jnp.float32)
                total = p if total is None else total + p
    return total


def natural(me_ref, near_ref, far_ref, texts_ref):
    n, step, _ = near_ref.shape
    core, y = me_ref[0], me_ref[1]
    for k, there in enumerate(pairs(y, -1, n)):
        for other, ref in enumerate((near_ref, far_ref)):
            at = (there * 2 + (core ^ other)) * step
            texts_ref[pl.ds(pl.multiple_of(at, step), step), :] = ref[k]


def pairs(y, way, n):
    two = y + way * (2 - 4 * (y & 1))
    return [(at + half) & (n - 1) for at in (y, y + way, y - way, two) for half in (0, n // 2)]


def logits_kernel(
    me_ref, allow_ref, images_ref, near_ref, far_ref, logits_ref, row_ref, col_ref, texts_ref
):
    width, rows = images_ref.shape
    cols = texts_ref.shape[1]
    inv = width ** (-0.5)
    natural(me_ref, near_ref, far_ref, texts_ref)
    texts = split(texts_ref[...].T, 3)
    for i in range(rows // BLK):
        at = pl.ds(i * BLK, BLK)
        part = product(texts, split(images_ref[:, at], 3), NN, 2) * inv
        for j in range(cols // BLK):
            block = jnp.where(allow_ref[i, j] > 0, part[j * BLK : (j + 1) * BLK], NEG)
            logits_ref[pl.ds(j * BLK, BLK), at] = block
        part = logits_ref[:, at]
        top = jnp.max(part, axis=0, keepdims=True)
        lse = top + jnp.log(jnp.sum(jnp.exp(part - top), axis=0, keepdims=True))
        put(row_ref, lse, i * BLK // LANES)
    for j in range(cols // BLK):
        part = logits_ref[pl.ds(j * BLK, BLK), :]
        top = jnp.max(part, axis=1, keepdims=True)
        lse = top + jnp.log(jnp.sum(jnp.exp(part - top), axis=1, keepdims=True))
        lse = jnp.broadcast_to(lse, (BLK, LANES)).T[:1]
        for first in range(j * BLK // LANES, col_ref.shape[1], cols // LANES):
            put(col_ref, lse, first)


def put(ref, values, first):
    for k in range(values.shape[1] // LANES):
        row = values[:, k * LANES : (k + 1) * LANES]
        ref[:, pl.ds(first + k, 1), :] = jnp.broadcast_to(row[None], (ref.shape[0], 1, LANES))


def lse_of(parts):
    top = jnp.max(parts, axis=0)
    return top + jnp.log(jnp.sum(jnp.exp(parts - top[None]), axis=0))


def gradient(me_ref, logits_ref, row_ref, col_ref):
    cols, rows = logits_ref.shape
    row_lse = lse_of(row_ref[...])
    col_lse = lse_of(col_ref[...])
    col_lse = jnp.concatenate(
        [jnp.broadcast_to(col_lse[k : k + 1], (LANES, LANES)).T[:, :1] for k in range(cols // LANES)]
    )
    ahead = me_ref[2] - me_ref[3]
    for i in range(rows // BLK):
        part = logits_ref[:, pl.ds(i * BLK, BLK)]
        first = i * BLK // LANES
        row = jnp.concatenate([row_lse[first + k : first + k + 1] for k in range(BLK // LANES)], axis=1)
        grad = 0.5 * (jnp.exp(part - row) + jnp.exp(part - col_lse))
        text_at = lax.broadcasted_iota(jnp.int32, grad.shape, 0)
        image_at = lax.broadcasted_iota(jnp.int32, grad.shape, 1) + (i * BLK + ahead)
        yield pl.ds(i * BLK, BLK), jnp.where(text_at == image_at, grad - 1.0, grad)


def image_kernel(me_ref, logits_ref, row_ref, col_ref, near_ref, far_ref, terms_ref, texts_ref):
    inv = texts_ref.shape[0] ** (-0.5)
    natural(me_ref, near_ref, far_ref, texts_ref)
    texts = split(texts_ref[...], 2)
    for at, grad in gradient(me_ref, logits_ref, row_ref, col_ref):
        terms_ref[:, at] = product(texts, split(grad, 2), NN, 1) * inv


def text_kernel(me_ref, logits_ref, row_ref, col_ref, images_ref, keep_ref, send_ref, all_ref):
    inv = images_ref.shape[0] ** (-0.5)
    total = None
    for at, grad in gradient(me_ref, logits_ref, row_ref, col_ref):
        p = product(split(images_ref[:, at], 2), split(grad, 2), NT, 1)
        total = p if total is None else total + p
    all_ref[...] = total * inv
    n, step, _ = keep_ref.shape
    core, y = me_ref[0], me_ref[1]
    for k, there in enumerate(pairs(y, 1, n)):
        for other, ref in enumerate((keep_ref, send_ref)):
            at = (there * 2 + (core ^ other)) * step
            ref[k] = all_ref[pl.ds(pl.multiple_of(at, step), step), :]


def sum_kernel(parts_in, after_ref, out_ref, parts_ref, sems):
    del after_ref
    loads = [
        pltpu.make_async_copy(parts_in.at[k], parts_ref.at[k], sems.at[k]) for k in range(parts_in.shape[0])
    ]
    for load in loads:
        load.start()
    for load in loads:
        load.wait()
    out_ref[...] = jnp.sum(parts_ref[...], axis=0)


def gather(block, axis, n):
    return lax.all_to_all(jnp.broadcast_to(block[None], (n,) + block.shape), axis, 0, 0)


def after(x, y):
    return x + 0.0 * y.reshape(-1)[0]


def sum_of(parts, after):
    return pl.pallas_call(
        sum_kernel,
        out_shape=jax.ShapeDtypeStruct(parts.shape[1:], parts.dtype),
        in_specs=[ANY, ANY],
        scratch_shapes=[pltpu.VMEM(parts.shape, parts.dtype), pltpu.SemaphoreType.DMA((parts.shape[0],))],
        compiler_params=PARAMS,
        name="sum",
    )(parts, after)


def flip(n, bit):
    return [(i, i ^ bit) for i in range(n)]


def shifts(n):
    return [
        [(i, (i + 1) % n) for i in range(n)],
        [(i, (i - 1) % n) for i in range(n)],
        [(i, (i + 2 - 4 * (i % 2)) % n) for i in range(n)],
    ]


def body(image_embeddings, text_embeddings, negatives_mask):
    ny, nc, nx, nz = (lax.axis_size(a) for a in ("y", "core", "x", "z"))
    rows, own = image_embeddings.shape
    cols, own_text = text_embeddings.shape
    texts = text_embeddings.T
    far_half = lax.ppermute(texts, "y", flip(ny, ny // 2))
    images = gather(image_embeddings.T, "z", nz).reshape(nz * own, rows)
    texts = after(jnp.stack([texts, far_half]), images)
    images = gather(after(images, far_half), "x", nx).reshape(nx * nz * own, rows)
    near = jnp.concatenate([texts] + [lax.ppermute(texts, "y", perm) for perm in shifts(ny)])
    far = lax.ppermute(near, "core", flip(nc, 1))
    width = images.shape[0]
    row_start = lax.axis_index(ROW) * rows
    col_start = lax.axis_index(COL) * cols
    row_blocks, col_blocks = rows // BLK, cols // BLK
    first_row, first_col = row_start // BLK, col_start // BLK
    window = lax.dynamic_slice(negatives_mask, (first_row, first_col), (row_blocks, col_blocks))
    row_ids = first_row + jnp.arange(row_blocks, dtype=jnp.int32)
    col_ids = first_col + jnp.arange(col_blocks, dtype=jnp.int32)
    allow = ((window > 0) | (row_ids[:, None] == col_ids[None, :])).astype(jnp.int32)
    f32 = jnp.float32
    passes = 2 * rows * cols * width
    me = [lax.axis_index("core"), lax.axis_index("y"), row_start, col_start]
    me = jnp.stack(me).astype(jnp.int32)
    logits, row_parts, col_parts = pl.pallas_call(
        logits_kernel,
        out_shape=(
            jax.ShapeDtypeStruct((cols, rows), f32),
            jax.ShapeDtypeStruct((nx * nz, rows // LANES, LANES), f32),
            jax.ShapeDtypeStruct((ny * nc, rows // LANES, LANES), f32),
        ),
        in_specs=[SMEM, SMEM, VMEM, VMEM, VMEM],
        out_specs=(VMEM, VMEM, VMEM),
        scratch_shapes=[pltpu.VMEM((width, cols), f32)],
        compiler_params=PARAMS,
        cost_estimate=pl.CostEstimate(flops=6 * passes, bytes_accessed=5 << 20, transcendentals=0),
        name="logits",
    )(me, allow, images, near, far)
    col_parts = lax.all_to_all(col_parts, ROW, 0, 0)
    row_parts = lax.all_to_all(row_parts, COL, 0, 0)
    image_terms = pl.pallas_call(
        image_kernel,
        out_shape=jax.ShapeDtypeStruct((width, rows), f32),
        in_specs=[SMEM, VMEM, VMEM, VMEM, VMEM, VMEM],
        out_specs=VMEM,
        scratch_shapes=[pltpu.VMEM((width, cols), f32)],
        compiler_params=PARAMS,
        cost_estimate=pl.CostEstimate(flops=3 * passes, bytes_accessed=5 << 20, transcendentals=0),
        name="image_terms",
    )(me, logits, row_parts, col_parts, near, far)
    half = jax.ShapeDtypeStruct((ny, own_text, cols), f32)
    keep, send = pl.pallas_call(
        text_kernel,
        out_shape=(half, half),
        in_specs=[SMEM, VMEM, VMEM, VMEM, VMEM],
        out_specs=(VMEM, VMEM),
        scratch_shapes=[pltpu.VMEM((width, cols), f32)],
        compiler_params=PARAMS,
        cost_estimate=pl.CostEstimate(flops=3 * passes, bytes_accessed=5 << 20, transcendentals=0),
        name="text_terms",
    )(me, logits, row_parts, col_parts, images)
    parts = lax.all_to_all(image_terms.reshape(nx, nz * own, rows), "x", 0, 0)
    grad_text = keep + lax.ppermute(send, "core", flip(nc, 1))
    grad_text = grad_text.reshape(4, 2, own_text, cols)
    moved = [lax.ppermute(grad_text[k + 1], "y", perm) for k, perm in enumerate(shifts(ny))]
    parts = sum_of(parts, moved[0] + moved[1])
    grad_text = sum(moved, grad_text[0])
    grad_text = grad_text[0] + lax.ppermute(grad_text[1], "y", flip(ny, ny // 2))
    grad_image = jnp.sum(lax.all_to_all(parts.reshape(nz, own, rows), "z", 0, 0), axis=0)
    return (grad_image.T, grad_text.T)


def solution(mesh):
    rows, cols = mesh.devices.shape
    fine = Mesh(mesh.devices.reshape(rows // 2, 2, 4, cols // 4), ("y", "core", "x", "z"))
    return jax.shard_map(
        body,
        mesh=fine,
        in_specs=(P(ROW, COL), P(COL, ROW), P()),
        out_specs=(P(ROW, COL), P(COL, ROW)),
        check_vma=False,
    )
```

```python
import functools

import jax
import jax.numpy as jnp
from jax import lax
from jax.experimental import pallas as pl
from jax.experimental.pallas import tpu as pltpu
from jax.sharding import Mesh
from jax.sharding import PartitionSpec as P

BLK = 256
LANES = 128
NEG = -1e30
Y = ("y_far", "y_near")
ROW = Y + ("core",)
COL = ("x", "z")
VMEM = pl.BlockSpec(memory_space=pltpu.VMEM)
HBM = pl.BlockSpec(memory_space=pltpu.HBM)
SMEM = pl.BlockSpec(memory_space=pltpu.SMEM)
ANY = pl.BlockSpec(memory_space=pl.ANY)
PARAMS = pltpu.CompilerParams(vmem_limit_bytes=40 * 2**20)
NN = (((1,), (0,)), ((), ()))
NT = (((1,), (1,)), ((), ()))


def split(x, terms):
    out = []
    for _ in range(terms):
        out.append(x.astype(jnp.bfloat16))
        x = x - out[-1].astype(jnp.float32)
    return out


def product(a, b, dims, order):
    total = None
    for both in range(order, -1, -1):
        for i in range(both + 1):
            if i < len(a) and both - i < len(b):
                p = lax.dot_general(a[i], b[both - i], dims, preferred_element_type=jnp.float32)
                total = p if total is None else total + p
    return total


def place(me_ref, there, core, step, chunk):
    shard = there * 2 + core
    per = chunk // step
    apart = (shard // per) ^ me_ref[4]
    first = 1 + me_ref[0]
    order = jnp.where(apart == 0, 0, jnp.where(apart == 1, first, jnp.where(apart == 3, 3 - first, 3)))
    return pl.ds(pl.multiple_of(order * chunk + (shard & (per - 1)) * step, step), step)


def arrange(me_ref, near_ref, far_ref, texts_ref):
    n, step, _ = near_ref.shape
    core, y = me_ref[0], me_ref[1]
    for k in range(n):
        there = (((y // (n // 2)) ^ (k % 2)) * (n // 2)) + k // 2
        for other, ref in enumerate((near_ref, far_ref)):
            texts_ref[place(me_ref, there, core ^ other, step, texts_ref.shape[0] // 4), :] = ref[k]


def pairs(y, way, n):
    two = y + way * (2 - 4 * (y & 1))
    return [(at + half) & (n - 1) for at in (y, y + way, y - way, two) for half in (0, n // 2)]


def logits_kernel(
    me_ref, allow_ref, own_ref, first_ref, second_ref, across_ref, near_ref, far_ref, logits_ref, row_ref, col_ref, texts_ref
):
    rows = own_ref.shape[1]
    width, cols = texts_ref.shape
    inv = width ** (-0.5)
    refs = (own_ref, first_ref, second_ref, across_ref)
    arrange(me_ref, near_ref, far_ref, texts_ref)
    texts = split(texts_ref[...].T, 3)
    for i in range(rows // BLK):
        at = pl.ds(i * BLK, BLK)
        images = jnp.concatenate([ref[:, at] for ref in refs])
        part = product(texts, split(images, 3), NN, 2) * inv
        for j in range(cols // BLK):
            block = jnp.where(allow_ref[i, j] > 0, part[j * BLK : (j + 1) * BLK], NEG)
            logits_ref[pl.ds(j * BLK, BLK), at] = block
        part = logits_ref[:, at]
        top = jnp.max(part, axis=0, keepdims=True)
        lse = top + jnp.log(jnp.sum(jnp.exp(part - top), axis=0, keepdims=True))
        put(row_ref, lse, i * BLK // LANES)
    for j in range(cols // BLK):
        part = logits_ref[pl.ds(j * BLK, BLK), :]
        top = jnp.max(part, axis=1, keepdims=True)
        lse = top + jnp.log(jnp.sum(jnp.exp(part - top), axis=1, keepdims=True))
        lse = jnp.broadcast_to(lse, (BLK, LANES)).T[:1]
        for first in range(j * BLK // LANES, col_ref.shape[1], cols // LANES):
            put(col_ref, lse, first)


def put(ref, values, first):
    for k in range(values.shape[1] // LANES):
        row = values[:, k * LANES : (k + 1) * LANES]
        ref[:, pl.ds(first + k, 1), :] = jnp.broadcast_to(row[None], (ref.shape[0], 1, LANES))


def lse_of(parts):
    top = jnp.max(parts, axis=0)
    return top + jnp.log(jnp.sum(jnp.exp(parts - top[None]), axis=0))


def gradient(me_ref, logits_ref, row_ref, col_ref):
    cols, rows = logits_ref.shape
    row_lse = lse_of(row_ref[...])
    col_lse = lse_of(col_ref[...])
    col_lse = jnp.concatenate(
        [jnp.broadcast_to(col_lse[k : k + 1], (LANES, LANES)).T[:, :1] for k in range(cols // LANES)]
    )
    ahead = me_ref[2] - me_ref[3]
    for i in range(rows // BLK):
        part = logits_ref[:, pl.ds(i * BLK, BLK)]
        first = i * BLK // LANES
        row = jnp.concatenate([row_lse[first + k : first + k + 1] for k in range(BLK // LANES)], axis=1)
        grad = 0.5 * (jnp.exp(part - row) + jnp.exp(part - col_lse))
        text_at = lax.broadcasted_iota(jnp.int32, grad.shape, 0)
        image_at = lax.broadcasted_iota(jnp.int32, grad.shape, 1) + (i * BLK + ahead)
        yield pl.ds(i * BLK, BLK), jnp.where(text_at == image_at, grad - 1.0, grad)


def image_kernel(
    me_ref, logits_ref, row_ref, col_ref, near_ref, far_ref, own_ref, first_ref, second_ref, across_ref, texts_ref
):
    inv = texts_ref.shape[0] ** (-0.5)
    arrange(me_ref, near_ref, far_ref, texts_ref)
    texts = split(texts_ref[...], 2)
    chunk = own_ref.shape[0]
    for at, grad in gradient(me_ref, logits_ref, row_ref, col_ref):
        terms = product(texts, split(grad, 2), NN, 1) * inv
        for k, ref in enumerate((own_ref, first_ref, second_ref, across_ref)):
            ref[:, at] = terms[k * chunk : (k + 1) * chunk]


def text_kernel(
    me_ref, logits_ref, row_ref, col_ref, own_ref, first_ref, second_ref, across_ref, keep_ref, send_ref, all_ref
):
    inv = all_ref.shape[0] ** (-0.5)
    refs = (own_ref, first_ref, second_ref, across_ref)
    total = None
    for at, grad in gradient(me_ref, logits_ref, row_ref, col_ref):
        images = jnp.concatenate([ref[:, at] for ref in refs])
        p = product(split(images, 2), split(grad, 2), NT, 1)
        total = p if total is None else total + p
    all_ref[...] = total * inv
    n, step, _ = keep_ref.shape
    core, y = me_ref[0], me_ref[1]
    for k, there in enumerate(pairs(y, 1, n)):
        for other, ref in enumerate((keep_ref, send_ref)):
            ref[k] = all_ref[place(me_ref, there, core ^ other, step, own_ref.shape[0]), :]


def sum_kernel(a_ref, b_ref, c_ref, after_ref, out_ref):
    del after_ref
    out_ref[...] = a_ref[...] + b_ref[...] + c_ref[...]


def gather(block, axis, n):
    return lax.all_to_all(jnp.broadcast_to(block[None], (n,) + block.shape), axis, 0, 0)


def after(x, y):
    return x + 0.0 * y[(0,) * y.ndim]


def sum_of(a, b, c, then):
    return pl.pallas_call(
        sum_kernel,
        out_shape=jax.ShapeDtypeStruct(a.shape, a.dtype),
        in_specs=[VMEM, VMEM, VMEM, ANY],
        compiler_params=PARAMS,
        name="sum",
    )(a, b, c, then)


def flip(n, bit):
    return [(i, i ^ bit) for i in range(n)]


def shifts(n):
    return [
        [(i, (i + 1) % n) for i in range(n)],
        [(i, (i - 1) % n) for i in range(n)],
        [(i, (i + 2 - 4 * (i % 2)) % n) for i in range(n)],
    ]


def neighbours(nx, nc):
    first, second = (1, 3), (3, 1)
    return [
        [(c * nx + x, c * nx + (x ^ apart[c])) for c in range(nc) for x in range(nx)]
        for apart in (first, second)
    ]


def body(image_embeddings, text_embeddings, negatives_mask):
    ny, nc, nx, nz = (lax.axis_size(a) for a in (Y, "core", "x", "z"))
    rows, own = image_embeddings.shape
    cols, own_text = text_embeddings.shape
    texts = text_embeddings.T
    far_half = lax.ppermute(texts, Y, flip(ny, ny // 2))
    images = gather(image_embeddings.T, "z", nz).reshape(nz * own, rows)
    texts = after(jnp.stack([texts, far_half]), images)
    images = after(images, far_half)
    to_first, to_second = neighbours(nx, nc)
    first = lax.ppermute(images, ("core", "x"), to_first)
    second = lax.ppermute(images, ("core", "x"), to_second)
    across = lax.ppermute(first, ("core", "x"), to_second)
    images = (images, first, second, across)
    near = gather(texts, "y_near", ny // 2).reshape(ny, own_text, cols)
    far = lax.ppermute(after(near, across), "core", flip(nc, 1))
    width = nx * nz * own
    row_start = lax.axis_index(ROW) * rows
    col_start = lax.axis_index(COL) * cols
    row_blocks, col_blocks = rows // BLK, cols // BLK
    first_row, first_col = row_start // BLK, col_start // BLK
    window = lax.dynamic_slice(negatives_mask, (first_row, first_col), (row_blocks, col_blocks))
    row_ids = first_row + jnp.arange(row_blocks, dtype=jnp.int32)
    col_ids = first_col + jnp.arange(col_blocks, dtype=jnp.int32)
    allow = ((window > 0) | (row_ids[:, None] == col_ids[None, :])).astype(jnp.int32)
    f32 = jnp.float32
    passes = 2 * rows * cols * width
    me = [lax.axis_index("core"), lax.axis_index(Y), row_start, col_start, lax.axis_index("x")]
    me = jnp.stack(me).astype(jnp.int32)
    logits, row_parts, col_parts = pl.pallas_call(
        logits_kernel,
        out_shape=(
            jax.ShapeDtypeStruct((cols, rows), f32),
            jax.ShapeDtypeStruct((nx * nz, rows // LANES, LANES), f32),
            jax.ShapeDtypeStruct((ny * nc, rows // LANES, LANES), f32),
        ),
        in_specs=[SMEM, SMEM] + [VMEM] * 6,
        out_specs=(VMEM, VMEM, VMEM),
        scratch_shapes=[pltpu.VMEM((width, cols), f32)],
        compiler_params=PARAMS,
        cost_estimate=pl.CostEstimate(flops=6 * passes, bytes_accessed=5 << 20, transcendentals=0),
        name="logits",
    )(me, allow, *images, near, far)
    col_parts = lax.all_to_all(col_parts, ROW, 0, 0)
    row_parts = lax.all_to_all(row_parts, COL, 0, 0)
    own_terms, first, second, across = pl.pallas_call(
        image_kernel,
        out_shape=(jax.ShapeDtypeStruct((nz * own, rows), f32),) * 4,
        in_specs=[SMEM] + [VMEM] * 5,
        out_specs=(VMEM,) * 4,
        scratch_shapes=[pltpu.VMEM((width, cols), f32)],
        compiler_params=PARAMS,
        cost_estimate=pl.CostEstimate(flops=3 * passes, bytes_accessed=5 << 20, transcendentals=0),
        name="image_terms",
    )(me, logits, row_parts, col_parts, near, far)
    half = jax.ShapeDtypeStruct((ny, own_text, cols), f32)
    keep, send = pl.pallas_call(
        text_kernel,
        out_shape=(half, half),
        in_specs=[SMEM] + [VMEM] * 7,
        out_specs=(VMEM, VMEM),
        scratch_shapes=[pltpu.VMEM((width, cols), f32)],
        compiler_params=PARAMS,
        cost_estimate=pl.CostEstimate(flops=3 * passes, bytes_accessed=5 << 20, transcendentals=0),
        name="text_terms",
    )(me, logits, row_parts, col_parts, *images)
    across = lax.ppermute(across, ("core", "x"), to_second)
    second = lax.ppermute(second, ("core", "x"), to_second)
    first = lax.ppermute(first + across, ("core", "x"), to_first)
    grad_text = keep + lax.ppermute(send, "core", flip(nc, 1))
    grad_text = grad_text.reshape(4, 2, own_text, cols)
    moved = [lax.ppermute(grad_text[k + 1], Y, perm) for k, perm in enumerate(shifts(ny))]
    parts = sum_of(own_terms, first, second, moved[0] + moved[1])
    grad_text = sum(moved, grad_text[0])
    grad_text = grad_text[0] + lax.ppermute(grad_text[1], Y, flip(ny, ny // 2))
    grad_image = jnp.sum(lax.all_to_all(parts.reshape(nz, own, rows), "z", 0, 0), axis=0)
    return (grad_image.T, grad_text.T)


def solution(mesh):
    rows, cols = mesh.devices.shape
    fine = Mesh(mesh.devices.reshape(2, rows // 4, 2, 4, cols // 4), ROW + COL)
    return jax.shard_map(
        body,
        mesh=fine,
        in_specs=(P(ROW, COL), P(COL, ROW), P()),
        out_specs=(P(ROW, COL), P(COL, ROW)),
        check_vma=False,
    )
```

```python
import functools

import jax
import jax.numpy as jnp
from jax import lax
from jax.experimental import pallas as pl
from jax.experimental.pallas import tpu as pltpu
from jax.sharding import Mesh
from jax.sharding import PartitionSpec as P

BLK = 256
LANES = 128
NEG = -1e30
Y = ("y_far", "y_near")
ROW = Y + ("core",)
COL = ("x", "z")
VMEM = pl.BlockSpec(memory_space=pltpu.VMEM)
HBM = pl.BlockSpec(memory_space=pltpu.HBM)
SMEM = pl.BlockSpec(memory_space=pltpu.SMEM)
ANY = pl.BlockSpec(memory_space=pl.ANY)
PARAMS = pltpu.CompilerParams(vmem_limit_bytes=24 * 2**20)
NN = (((1,), (0,)), ((), ()))
NT = (((1,), (1,)), ((), ()))


def split(x, terms):
    out = []
    for _ in range(terms):
        out.append(x.astype(jnp.bfloat16))
        x = x - out[-1].astype(jnp.float32)
    return out


def product(a, b, dims, order):
    total = None
    for both in range(order, -1, -1):
        for i in range(both + 1):
            if i < len(a) and both - i < len(b):
                p = lax.dot_general(a[i], b[both - i], dims, preferred_element_type=jnp.float32)
                total = p if total is None else total + p
    return total


def place(me_ref, there, core, step, chunk):
    shard = there * 2 + core
    per = chunk // step
    apart = (shard // per) ^ me_ref[4]
    first = 1 + me_ref[0]
    order = jnp.where(apart == 0, 0, jnp.where(apart == 1, first, jnp.where(apart == 3, 3 - first, 3)))
    return pl.ds(pl.multiple_of(order * chunk + (shard & (per - 1)) * step, step), step)


def arrange(me_ref, near_ref, far_ref, texts_ref):
    n, step, _ = near_ref.shape
    core, y = me_ref[0], me_ref[1]
    for k in range(n):
        there = (((y // (n // 2)) ^ (k % 2)) * (n // 2)) + k // 2
        for other, ref in enumerate((near_ref, far_ref)):
            texts_ref[place(me_ref, there, core ^ other, step, texts_ref.shape[0] // 4), :] = ref[k]


def pairs(y, way, n):
    two = y + way * (2 - 4 * (y & 1))
    return [(at + half) & (n - 1) for at in (y, y + way, y - way, two) for half in (0, n // 2)]


def logits_kernel(
    me_ref, allow_ref, own_ref, first_ref, second_ref, across_ref, near_ref, far_ref, logits_ref, row_ref, col_ref, texts_ref
):
    rows = own_ref.shape[1]
    width, cols = texts_ref.shape
    inv = width ** (-0.5)
    refs = (own_ref, first_ref, second_ref, across_ref)
    arrange(me_ref, near_ref, far_ref, texts_ref)
    texts = split(texts_ref[...].T, 3)
    for i in range(rows // BLK):
        at = pl.ds(i * BLK, BLK)
        images = jnp.concatenate([ref[:, at] for ref in refs])
        part = product(texts, split(images, 3), NN, 2) * inv
        for j in range(cols // BLK):
            block = jnp.where(allow_ref[i, j] > 0, part[j * BLK : (j + 1) * BLK], NEG)
            logits_ref[pl.ds(j * BLK, BLK), at] = block
        part = logits_ref[:, at]
        top = jnp.max(part, axis=0, keepdims=True)
        lse = top + jnp.log(jnp.sum(jnp.exp(part - top), axis=0, keepdims=True))
        put(row_ref, lse, i * BLK // LANES)
    for j in range(cols // BLK):
        part = logits_ref[pl.ds(j * BLK, BLK), :]
        top = jnp.max(part, axis=1, keepdims=True)
        lse = top + jnp.log(jnp.sum(jnp.exp(part - top), axis=1, keepdims=True))
        lse = jnp.broadcast_to(lse, (BLK, LANES)).T[:1]
        for first in range(j * BLK // LANES, col_ref.shape[1], cols // LANES):
            put(col_ref, lse, first)


def put(ref, values, first):
    for k in range(values.shape[1] // LANES):
        row = values[:, k * LANES : (k + 1) * LANES]
        ref[:, pl.ds(first + k, 1), :] = jnp.broadcast_to(row[None], (ref.shape[0], 1, LANES))


def lse_of(parts):
    top = jnp.max(parts, axis=0)
    return top + jnp.log(jnp.sum(jnp.exp(parts - top[None]), axis=0))


def gradient(me_ref, logits_ref, row_ref, col_ref):
    cols, rows = logits_ref.shape
    row_lse = lse_of(row_ref[...])
    col_lse = lse_of(col_ref[...])
    col_lse = jnp.concatenate(
        [jnp.broadcast_to(col_lse[k : k + 1], (LANES, LANES)).T[:, :1] for k in range(cols // LANES)]
    )
    ahead = me_ref[2] - me_ref[3]
    for i in range(rows // BLK):
        part = logits_ref[:, pl.ds(i * BLK, BLK)]
        first = i * BLK // LANES
        row = jnp.concatenate([row_lse[first + k : first + k + 1] for k in range(BLK // LANES)], axis=1)
        grad = 0.5 * (jnp.exp(part - row) + jnp.exp(part - col_lse))
        text_at = lax.broadcasted_iota(jnp.int32, grad.shape, 0)
        image_at = lax.broadcasted_iota(jnp.int32, grad.shape, 1) + (i * BLK + ahead)
        yield pl.ds(i * BLK, BLK), jnp.where(text_at == image_at, grad - 1.0, grad)


def image_kernel(
    me_ref, logits_ref, row_ref, col_ref, near_ref, far_ref, own_ref, first_ref, second_ref, across_ref, high_ref, low_ref,
    texts_ref,
):
    inv = texts_ref.shape[0] ** (-0.5)
    arrange(me_ref, near_ref, far_ref, texts_ref)
    texts = split(texts_ref[...], 2)
    chunk = own_ref.shape[0]
    for at, grad in gradient(me_ref, logits_ref, row_ref, col_ref):
        high, low = split(grad, 2)
        high_ref[:, at] = high
        low_ref[:, at] = low
        terms = product(texts, [high, low], NN, 1) * inv
        for k, ref in enumerate((own_ref, first_ref, second_ref, across_ref)):
            ref[:, at] = terms[k * chunk : (k + 1) * chunk]


def text_kernel(
    me_ref, high_ref, low_ref, own_ref, first_ref, second_ref, across_ref, keep_ref, send_ref, all_ref
):
    inv = all_ref.shape[0] ** (-0.5)
    images = jnp.concatenate([ref[...] for ref in (own_ref, first_ref, second_ref, across_ref)])
    total = product(split(images, 2), [high_ref[...], low_ref[...]], NT, 1)
    all_ref[...] = total * inv
    n, step, _ = keep_ref.shape
    core, y = me_ref[0], me_ref[1]
    for k, there in enumerate(pairs(y, 1, n)):
        for other, ref in enumerate((keep_ref, send_ref)):
            ref[k] = all_ref[place(me_ref, there, core ^ other, step, own_ref.shape[0]), :]


def sum_kernel(a_ref, b_ref, c_ref, after_ref, out_ref):
    del after_ref
    out_ref[...] = a_ref[...] + b_ref[...] + c_ref[...]


def gather(block, axis, n):
    return lax.all_to_all(jnp.broadcast_to(block[None], (n,) + block.shape), axis, 0, 0)


def after(x, *others):
    return pl.pallas_call(
        lambda *refs: None,
        out_shape=jax.ShapeDtypeStruct(x.shape, x.dtype),
        in_specs=[ANY] * (1 + len(others)),
        out_specs=ANY,
        input_output_aliases={0: 0},
        compiler_params=PARAMS,
        name="after",
    )(x, *others)


def sum_of(a, b, c, then):
    return pl.pallas_call(
        sum_kernel,
        out_shape=jax.ShapeDtypeStruct(a.shape, a.dtype),
        in_specs=[VMEM, VMEM, VMEM, ANY],
        compiler_params=PARAMS,
        name="sum",
    )(a, b, c, then)


def flip(n, bit):
    return [(i, i ^ bit) for i in range(n)]


def shifts(n):
    return [
        [(i, (i + 1) % n) for i in range(n)],
        [(i, (i - 1) % n) for i in range(n)],
        [(i, (i + 2 - 4 * (i % 2)) % n) for i in range(n)],
    ]


def neighbours(nx, nc):
    first, second = (1, 3), (3, 1)
    return [
        [(c * nx + x, c * nx + (x ^ apart[c])) for c in range(nc) for x in range(nx)]
        for apart in (first, second)
    ]


def body(image_embeddings, text_embeddings, negatives_mask):
    ny, nc, nx, nz = (lax.axis_size(a) for a in (Y, "core", "x", "z"))
    rows, own = image_embeddings.shape
    cols, own_text = text_embeddings.shape
    texts = text_embeddings.T
    far_half = lax.ppermute(texts, Y, flip(ny, ny // 2))
    images = gather(image_embeddings.T, "z", nz).reshape(nz * own, rows)
    texts = after(jnp.stack([texts, far_half]), images)
    images = after(images, far_half)
    to_first, to_second = neighbours(nx, nc)
    first = lax.ppermute(images, ("core", "x"), to_first)
    second = lax.ppermute(images, ("core", "x"), to_second)
    across = lax.ppermute(first, ("core", "x"), to_second)
    images = (images, first, second, across)
    near = gather(texts, "y_near", ny // 2).reshape(ny, own_text, cols)
    far = lax.ppermute(near + 0.0 * across[0, 0], "core", flip(nc, 1))
    width = nx * nz * own
    row_start = lax.axis_index(ROW) * rows
    col_start = lax.axis_index(COL) * cols
    row_blocks, col_blocks = rows // BLK, cols // BLK
    first_row, first_col = row_start // BLK, col_start // BLK
    window = lax.dynamic_slice(negatives_mask, (first_row, first_col), (row_blocks, col_blocks))
    row_ids = first_row + jnp.arange(row_blocks, dtype=jnp.int32)
    col_ids = first_col + jnp.arange(col_blocks, dtype=jnp.int32)
    allow = ((window > 0) | (row_ids[:, None] == col_ids[None, :])).astype(jnp.int32)
    f32 = jnp.float32
    passes = 2 * rows * cols * width
    me = [lax.axis_index("core"), lax.axis_index(Y), row_start, col_start, lax.axis_index("x")]
    me = jnp.stack(me).astype(jnp.int32)
    logits, row_parts, col_parts = pl.pallas_call(
        logits_kernel,
        out_shape=(
            jax.ShapeDtypeStruct((cols, rows), f32),
            jax.ShapeDtypeStruct((nx * nz, rows // LANES, LANES), f32),
            jax.ShapeDtypeStruct((ny * nc, rows // LANES, LANES), f32),
        ),
        in_specs=[SMEM, SMEM] + [VMEM] * 6,
        out_specs=(VMEM, VMEM, VMEM),
        scratch_shapes=[pltpu.VMEM((width, cols), f32)],
        compiler_params=PARAMS,
        cost_estimate=pl.CostEstimate(flops=6 * passes, bytes_accessed=5 << 20, transcendentals=0),
        name="logits",
    )(me, allow, *images, near, far)
    col_parts = lax.all_to_all(col_parts, ROW, 0, 0)
    row_parts = lax.all_to_all(row_parts, COL, 0, 0)
    own_terms, first, second, across, high, low = pl.pallas_call(
        image_kernel,
        out_shape=(jax.ShapeDtypeStruct((nz * own, rows), f32),) * 4
        + (jax.ShapeDtypeStruct((cols, rows), jnp.bfloat16),) * 2,
        in_specs=[SMEM] + [VMEM] * 5,
        out_specs=(VMEM,) * 6,
        scratch_shapes=[pltpu.VMEM((width, cols), f32)],
        compiler_params=PARAMS,
        cost_estimate=pl.CostEstimate(flops=3 * passes, bytes_accessed=5 << 20, transcendentals=0),
        name="image_terms",
    )(me, logits, row_parts, col_parts, near, far)
    half = jax.ShapeDtypeStruct((ny, own_text, cols), f32)
    keep, send = pl.pallas_call(
        text_kernel,
        out_shape=(half, half),
        in_specs=[SMEM] + [VMEM] * 6,
        out_specs=(VMEM, VMEM),
        scratch_shapes=[pltpu.VMEM((width, cols), f32)],
        compiler_params=PARAMS,
        cost_estimate=pl.CostEstimate(flops=3 * passes, bytes_accessed=5 << 20, transcendentals=0),
        name="text_terms",
    )(me, high, low, *images)
    across = lax.ppermute(across, ("core", "x"), to_second)
    second = lax.ppermute(second, ("core", "x"), to_second)
    first = lax.ppermute(first + across, ("core", "x"), to_first)
    grad_text = keep + lax.ppermute(send, "core", flip(nc, 1))
    grad_text = grad_text.reshape(4, 2, own_text, cols)
    moved = [lax.ppermute(grad_text[k + 1], Y, perm) for k, perm in enumerate(shifts(ny))]
    parts = sum_of(own_terms, first, second, moved[0] + moved[1])
    grad_text = sum(moved, grad_text[0])
    grad_text = grad_text[0] + lax.ppermute(grad_text[1], Y, flip(ny, ny // 2))
    grad_image = jnp.sum(lax.all_to_all(parts.reshape(nz, own, rows), "z", 0, 0), axis=0)
    return (grad_image.T, grad_text.T)


def solution(mesh):
    rows, cols = mesh.devices.shape
    fine = Mesh(mesh.devices.reshape(2, rows // 4, 2, 4, cols // 4), ROW + COL)
    return jax.shard_map(
        body,
        mesh=fine,
        in_specs=(P(ROW, COL), P(COL, ROW), P()),
        out_specs=(P(ROW, COL), P(COL, ROW)),
        check_vma=False,
    )
```

```python
import functools

import jax
import jax.numpy as jnp
from jax import lax
from jax.experimental import pallas as pl
from jax.experimental.pallas import tpu as pltpu
from jax.sharding import Mesh
from jax.sharding import PartitionSpec as P

BLK = 256
LANES = 128
NEG = -1e30
Y = ("y_far", "y_near")
ROW = Y + ("core",)
COL = ("x", "z")
VMEM = pl.BlockSpec(memory_space=pltpu.VMEM)
HBM = pl.BlockSpec(memory_space=pltpu.HBM)
SMEM = pl.BlockSpec(memory_space=pltpu.SMEM)
ANY = pl.BlockSpec(memory_space=pl.ANY)
PARAMS = pltpu.CompilerParams(vmem_limit_bytes=24 * 2**20)
NN = (((1,), (0,)), ((), ()))
NT = (((1,), (1,)), ((), ()))


def split(x, terms):
    out = []
    for _ in range(terms):
        out.append(x.astype(jnp.bfloat16))
        x = x - out[-1].astype(jnp.float32)
    return out


def product(a, b, dims, order):
    total = None
    for both in range(order, -1, -1):
        for i in range(both + 1):
            if i < len(a) and both - i < len(b):
                p = lax.dot_general(a[i], b[both - i], dims, preferred_element_type=jnp.float32)
                total = p if total is None else total + p
    return total


def place(me_ref, there, core, step, chunk):
    shard = there * 2 + core
    per = chunk // step
    apart = (shard // per) ^ me_ref[4]
    first = 1 + me_ref[0]
    order = jnp.where(apart == 0, 0, jnp.where(apart == 1, first, jnp.where(apart == 3, 3 - first, 3)))
    return pl.ds(pl.multiple_of(order * chunk + (shard & (per - 1)) * step, step), step)


def arrange(me_ref, near_ref, far_ref, texts_ref):
    n, step, _ = near_ref.shape
    core, y = me_ref[0], me_ref[1]
    for k in range(n):
        there = (((y // (n // 2)) ^ (k % 2)) * (n // 2)) + k // 2
        for other, ref in enumerate((near_ref, far_ref)):
            texts_ref[place(me_ref, there, core ^ other, step, texts_ref.shape[0] // 4), :] = ref[k]


def pairs(y, way, n):
    two = y + way * (2 - 4 * (y & 1))
    return [(at + half) & (n - 1) for at in (y, y + way, y - way, two) for half in (0, n // 2)]


def logits_kernel(
    me_ref, allow_ref, own_ref, first_ref, second_ref, across_ref, near_ref, far_ref,
    logits_ref, row_ref, col_ref, images_high_ref, images_low_ref, texts_high_ref, texts_low_ref, texts_ref,
):
    rows = own_ref.shape[1]
    width, cols = texts_ref.shape
    inv = width ** (-0.5)
    arrange(me_ref, near_ref, far_ref, texts_ref)
    texts_high_ref[...], texts_low_ref[...] = split(texts_ref[...], 2)
    texts = split(texts_ref[...].T, 3)
    for i in range(rows // BLK):
        at = pl.ds(i * BLK, BLK)
        images = jnp.concatenate([ref[:, at] for ref in (own_ref, first_ref, second_ref, across_ref)])
        images = split(images, 3)
        images_high_ref[:, at] = images[0]
        images_low_ref[:, at] = images[1]
        part = product(texts, images, NN, 2) * inv
        for j in range(cols // BLK):
            block = jnp.where(allow_ref[i, j] > 0, part[j * BLK : (j + 1) * BLK], NEG)
            logits_ref[pl.ds(j * BLK, BLK), at] = block
        part = logits_ref[:, at]
        top = jnp.max(part, axis=0, keepdims=True)
        lse = top + jnp.log(jnp.sum(jnp.exp(part - top), axis=0, keepdims=True))
        put(row_ref, lse, i * BLK // LANES)
    for j in range(cols // BLK):
        part = logits_ref[pl.ds(j * BLK, BLK), :]
        top = jnp.max(part, axis=1, keepdims=True)
        lse = top + jnp.log(jnp.sum(jnp.exp(part - top), axis=1, keepdims=True))
        lse = jnp.broadcast_to(lse, (BLK, LANES)).T[:1]
        for first in range(j * BLK // LANES, col_ref.shape[1], cols // LANES):
            put(col_ref, lse, first)


def put(ref, values, first):
    for k in range(values.shape[1] // LANES):
        row = values[:, k * LANES : (k + 1) * LANES]
        ref[:, pl.ds(first + k, 1), :] = jnp.broadcast_to(row[None], (ref.shape[0], 1, LANES))


def lse_of(parts):
    top = jnp.max(parts, axis=0)
    return top + jnp.log(jnp.sum(jnp.exp(parts - top[None]), axis=0))


def gradient(me_ref, logits_ref, row_ref, col_ref):
    cols, rows = logits_ref.shape
    row_lse = lse_of(row_ref[...])
    col_lse = lse_of(col_ref[...])
    col_lse = jnp.concatenate(
        [jnp.broadcast_to(col_lse[k : k + 1], (LANES, LANES)).T[:, :1] for k in range(cols // LANES)]
    )
    ahead = me_ref[2] - me_ref[3]
    for i in range(rows // BLK):
        part = logits_ref[:, pl.ds(i * BLK, BLK)]
        first = i * BLK // LANES
        row = jnp.concatenate([row_lse[first + k : first + k + 1] for k in range(BLK // LANES)], axis=1)
        grad = 0.5 * (jnp.exp(part - row) + jnp.exp(part - col_lse))
        text_at = lax.broadcasted_iota(jnp.int32, grad.shape, 0)
        image_at = lax.broadcasted_iota(jnp.int32, grad.shape, 1) + (i * BLK + ahead)
        yield pl.ds(i * BLK, BLK), jnp.where(text_at == image_at, grad - 1.0, grad)


def image_kernel(
    me_ref, logits_ref, row_ref, col_ref, texts_high_ref, texts_low_ref,
    own_ref, first_ref, second_ref, across_ref, high_ref, low_ref,
):
    inv = texts_high_ref.shape[0] ** (-0.5)
    texts = [texts_high_ref[...], texts_low_ref[...]]
    chunk = own_ref.shape[0]
    for at, grad in gradient(me_ref, logits_ref, row_ref, col_ref):
        high, low = split(grad, 2)
        high_ref[:, at] = high
        low_ref[:, at] = low
        terms = product(texts, [high, low], NN, 1) * inv
        for k, ref in enumerate((own_ref, first_ref, second_ref, across_ref)):
            ref[:, at] = terms[k * chunk : (k + 1) * chunk]


def text_kernel(me_ref, high_ref, low_ref, images_high_ref, images_low_ref, keep_ref, send_ref, all_ref):
    inv = all_ref.shape[0] ** (-0.5)
    images = [images_high_ref[...], images_low_ref[...]]
    total = product(images, [high_ref[...], low_ref[...]], NT, 1)
    all_ref[...] = total * inv
    n, step, _ = keep_ref.shape
    core, y = me_ref[0], me_ref[1]
    for k, there in enumerate(pairs(y, 1, n)):
        for other, ref in enumerate((keep_ref, send_ref)):
            ref[k] = all_ref[place(me_ref, there, core ^ other, step, all_ref.shape[0] // 4), :]


def sum_kernel(a_ref, b_ref, c_ref, after_ref, out_ref):
    del after_ref
    out_ref[...] = a_ref[...] + b_ref[...] + c_ref[...]


def gather(block, axis, n):
    return lax.all_to_all(jnp.broadcast_to(block[None], (n,) + block.shape), axis, 0, 0)


def after(x, *others):
    return pl.pallas_call(
        lambda *refs: None,
        out_shape=jax.ShapeDtypeStruct(x.shape, x.dtype),
        in_specs=[ANY] * (1 + len(others)),
        out_specs=ANY,
        input_output_aliases={0: 0},
        compiler_params=PARAMS,
        name="after",
    )(x, *others)


def sum_of(a, b, c, then):
    return pl.pallas_call(
        sum_kernel,
        out_shape=jax.ShapeDtypeStruct(a.shape, a.dtype),
        in_specs=[VMEM, VMEM, VMEM, ANY],
        compiler_params=PARAMS,
        name="sum",
    )(a, b, c, then)


def flip(n, bit):
    return [(i, i ^ bit) for i in range(n)]


def shifts(n):
    return [
        [(i, (i + 1) % n) for i in range(n)],
        [(i, (i - 1) % n) for i in range(n)],
        [(i, (i + 2 - 4 * (i % 2)) % n) for i in range(n)],
    ]


def neighbours(nx, nc):
    first, second = (1, 3), (3, 1)
    return [
        [(c * nx + x, c * nx + (x ^ apart[c])) for c in range(nc) for x in range(nx)]
        for apart in (first, second)
    ]


def body(image_embeddings, text_embeddings, negatives_mask):
    ny, nc, nx, nz = (lax.axis_size(a) for a in (Y, "core", "x", "z"))
    rows, own = image_embeddings.shape
    cols, own_text = text_embeddings.shape
    texts = text_embeddings.T
    far_half = lax.ppermute(texts, Y, flip(ny, ny // 2))
    images = gather(image_embeddings.T, "z", nz).reshape(nz * own, rows)
    texts = after(jnp.stack([texts, far_half]), images)
    images = after(images, far_half)
    to_first, to_second = neighbours(nx, nc)
    first = lax.ppermute(images, ("core", "x"), to_first)
    second = lax.ppermute(images, ("core", "x"), to_second)
    across = lax.ppermute(first, ("core", "x"), to_second)
    images = (images, first, second, across)
    near = gather(texts, "y_near", ny // 2).reshape(ny, own_text, cols)
    far = lax.ppermute(near + 0.0 * across[0, 0], "core", flip(nc, 1))
    width = nx * nz * own
    row_start = lax.axis_index(ROW) * rows
    col_start = lax.axis_index(COL) * cols
    row_blocks, col_blocks = rows // BLK, cols // BLK
    first_row, first_col = row_start // BLK, col_start // BLK
    window = lax.dynamic_slice(negatives_mask, (first_row, first_col), (row_blocks, col_blocks))
    row_ids = first_row + jnp.arange(row_blocks, dtype=jnp.int32)
    col_ids = first_col + jnp.arange(col_blocks, dtype=jnp.int32)
    allow = ((window > 0) | (row_ids[:, None] == col_ids[None, :])).astype(jnp.int32)
    f32, bf16 = jnp.float32, jnp.bfloat16
    passes = 2 * rows * cols * width
    me = [lax.axis_index("core"), lax.axis_index(Y), row_start, col_start, lax.axis_index("x")]
    me = jnp.stack(me).astype(jnp.int32)
    logits, row_parts, col_parts, images_high, images_low, texts_high, texts_low = pl.pallas_call(
        logits_kernel,
        out_shape=(
            jax.ShapeDtypeStruct((cols, rows), f32),
            jax.ShapeDtypeStruct((nx * nz, rows // LANES, LANES), f32),
            jax.ShapeDtypeStruct((ny * nc, rows // LANES, LANES), f32),
            jax.ShapeDtypeStruct((width, rows), bf16),
            jax.ShapeDtypeStruct((width, rows), bf16),
            jax.ShapeDtypeStruct((width, cols), bf16),
            jax.ShapeDtypeStruct((width, cols), bf16),
        ),
        in_specs=[SMEM, SMEM] + [VMEM] * 6,
        out_specs=(VMEM,) * 7,
        scratch_shapes=[pltpu.VMEM((width, cols), f32)],
        compiler_params=PARAMS,
        cost_estimate=pl.CostEstimate(flops=6 * passes, bytes_accessed=5 << 20, transcendentals=0),
        name="logits",
    )(me, allow, *images, near, far)
    col_parts = lax.all_to_all(col_parts, ROW, 0, 0)
    row_parts = lax.all_to_all(row_parts, COL, 0, 0)
    own_terms, first, second, across, high, low = pl.pallas_call(
        image_kernel,
        out_shape=(jax.ShapeDtypeStruct((nz * own, rows), f32),) * 4
        + (jax.ShapeDtypeStruct((cols, rows), bf16),) * 2,
        in_specs=[SMEM] + [VMEM] * 5,
        out_specs=(VMEM,) * 6,
        compiler_params=PARAMS,
        cost_estimate=pl.CostEstimate(flops=3 * passes, bytes_accessed=5 << 20, transcendentals=0),
        name="image_terms",
    )(me, logits, row_parts, col_parts, texts_high, texts_low)
    half = jax.ShapeDtypeStruct((ny, own_text, cols), f32)
    keep, send = pl.pallas_call(
        text_kernel,
        out_shape=(half, half),
        in_specs=[SMEM] + [VMEM] * 4,
        out_specs=(VMEM, VMEM),
        scratch_shapes=[pltpu.VMEM((width, cols), f32)],
        compiler_params=PARAMS,
        cost_estimate=pl.CostEstimate(flops=3 * passes, bytes_accessed=5 << 20, transcendentals=0),
        name="text_terms",
    )(me, high, low, images_high, images_low)
    across = lax.ppermute(across, ("core", "x"), to_second)
    second = lax.ppermute(second, ("core", "x"), to_second)
    first = lax.ppermute(first + across, ("core", "x"), to_first)
    grad_text = keep + lax.ppermute(send, "core", flip(nc, 1))
    grad_text = grad_text.reshape(4, 2, own_text, cols)
    moved = [lax.ppermute(grad_text[k + 1], Y, perm) for k, perm in enumerate(shifts(ny))]
    parts = sum_of(own_terms, first, second, moved[0] + moved[1])
    grad_text = sum(moved, grad_text[0])
    grad_text = grad_text[0] + lax.ppermute(grad_text[1], Y, flip(ny, ny // 2))
    grad_image = jnp.sum(lax.all_to_all(parts.reshape(nz, own, rows), "z", 0, 0), axis=0)
    return (grad_image.T, grad_text.T)


def solution(mesh):
    rows, cols = mesh.devices.shape
    fine = Mesh(mesh.devices.reshape(2, rows // 4, 2, 4, cols // 4), ROW + COL)
    return jax.shard_map(
        body,
        mesh=fine,
        in_specs=(P(ROW, COL), P(COL, ROW), P()),
        out_specs=(P(ROW, COL), P(COL, ROW)),
        check_vma=False,
    )
```

```python
import functools

import jax
import jax.numpy as jnp
from jax import lax
from jax.experimental import pallas as pl
from jax.experimental.pallas import tpu as pltpu
from jax.sharding import Mesh
from jax.sharding import PartitionSpec as P

BLK = 256
LANES = 128
NEG = -1e30
Y = ("y_far", "y_near")
ROW = Y + ("core",)
COL = ("x", "z")
VMEM = pl.BlockSpec(memory_space=pltpu.VMEM)
HBM = pl.BlockSpec(memory_space=pltpu.HBM)
SMEM = pl.BlockSpec(memory_space=pltpu.SMEM)
ANY = pl.BlockSpec(memory_space=pl.ANY)
PARAMS = pltpu.CompilerParams(vmem_limit_bytes=24 * 2**20)
NN = (((1,), (0,)), ((), ()))
NT = (((1,), (1,)), ((), ()))


def split(x, terms):
    out = []
    for _ in range(terms):
        out.append(x.astype(jnp.bfloat16))
        x = x - out[-1].astype(jnp.float32)
    return out


def product(a, b, dims, order):
    total = None
    for both in range(order, -1, -1):
        for i in range(both + 1):
            if i < len(a) and both - i < len(b):
                p = lax.dot_general(a[i], b[both - i], dims, preferred_element_type=jnp.float32)
                total = p if total is None else total + p
    return total


def place(me_ref, there, core, step, chunk):
    shard = there * 2 + core
    per = chunk // step
    apart = (shard // per) ^ me_ref[4]
    first = 1 + me_ref[0]
    order = jnp.where(apart == 0, 0, jnp.where(apart == 1, first, jnp.where(apart == 3, 3 - first, 3)))
    return pl.ds(pl.multiple_of(order * chunk + (shard & (per - 1)) * step, step), step)


def arrange(me_ref, near_ref, far_ref, texts_ref):
    n, step, _ = near_ref.shape
    core, y = me_ref[0], me_ref[1]
    for k in range(n):
        there = (((y // (n // 2)) ^ (k % 2)) * (n // 2)) + k // 2
        for other, ref in enumerate((near_ref, far_ref)):
            texts_ref[place(me_ref, there, core ^ other, step, texts_ref.shape[0] // 4), :] = ref[k]


def pairs(y, way, n):
    two = y + way * (2 - 4 * (y & 1))
    return [(at + half) & (n - 1) for at in (y, y + way, y - way, two) for half in (0, n // 2)]


def logits_kernel(
    me_ref, allow_ref, own_ref, first_ref, second_ref, across_ref, near_ref, far_ref,
    logits_ref, row_ref, col_ref, images_high_ref, images_low_ref, texts_high_ref, texts_low_ref, texts_ref,
):
    rows = own_ref.shape[1]
    width, cols = texts_ref.shape
    inv = width ** (-0.5)
    arrange(me_ref, near_ref, far_ref, texts_ref)
    texts_high_ref[...], texts_low_ref[...] = split(texts_ref[...], 2)
    texts = split(texts_ref[...].T, 3)
    for i in range(rows // BLK):
        at = pl.ds(i * BLK, BLK)
        images = jnp.concatenate([ref[:, at] for ref in (own_ref, first_ref, second_ref, across_ref)])
        images = split(images, 3)
        images_high_ref[:, at] = images[0]
        images_low_ref[:, at] = images[1]
        part = product(texts, images, NN, 2) * inv
        for j in range(cols // BLK):
            block = jnp.where(allow_ref[i, j] > 0, part[j * BLK : (j + 1) * BLK], NEG)
            logits_ref[pl.ds(j * BLK, BLK), at] = block
        part = logits_ref[:, at]
        top = jnp.max(part, axis=0, keepdims=True)
        lse = top + jnp.log(jnp.sum(jnp.exp(part - top), axis=0, keepdims=True))
        put(row_ref, lse, i * BLK // LANES)
    for j in range(cols // BLK):
        part = logits_ref[pl.ds(j * BLK, BLK), :]
        top = jnp.max(part, axis=1, keepdims=True)
        lse = top + jnp.log(jnp.sum(jnp.exp(part - top), axis=1, keepdims=True))
        lse = jnp.broadcast_to(lse, (BLK, LANES)).T[:1]
        for first in range(j * BLK // LANES, col_ref.shape[1], cols // LANES):
            put(col_ref, lse, first)


def put(ref, values, first):
    for k in range(values.shape[1] // LANES):
        row = values[:, k * LANES : (k + 1) * LANES]
        ref[:, pl.ds(first + k, 1), :] = jnp.broadcast_to(row[None], (ref.shape[0], 1, LANES))


def lse_of(parts):
    top = jnp.max(parts, axis=0)
    return top + jnp.log(jnp.sum(jnp.exp(parts - top[None]), axis=0))


def gradient(me_ref, logits_ref, row_ref, col_ref):
    cols, rows = logits_ref.shape
    row_lse = lse_of(row_ref[...])
    col_lse = lse_of(col_ref[...])
    col_lse = jnp.concatenate(
        [jnp.broadcast_to(col_lse[k : k + 1], (LANES, LANES)).T[:, :1] for k in range(cols // LANES)]
    )
    ahead = me_ref[2] - me_ref[3]
    for i in range(rows // BLK):
        part = logits_ref[:, pl.ds(i * BLK, BLK)]
        first = i * BLK // LANES
        row = jnp.concatenate([row_lse[first + k : first + k + 1] for k in range(BLK // LANES)], axis=1)
        grad = 0.5 * (jnp.exp(part - row) + jnp.exp(part - col_lse))
        text_at = lax.broadcasted_iota(jnp.int32, grad.shape, 0)
        image_at = lax.broadcasted_iota(jnp.int32, grad.shape, 1) + (i * BLK + ahead)
        yield pl.ds(i * BLK, BLK), jnp.where(text_at == image_at, grad - 1.0, grad)


def image_kernel(
    me_ref, logits_ref, row_ref, col_ref, texts_high_ref, texts_low_ref,
    own_ref, first_ref, second_ref, across_ref, high_ref, low_ref,
):
    inv = texts_high_ref.shape[0] ** (-0.5)
    texts = [texts_high_ref[...], texts_low_ref[...]]
    chunk = own_ref.shape[0]
    for at, grad in gradient(me_ref, logits_ref, row_ref, col_ref):
        high, low = split(grad, 2)
        high_ref[:, at] = high
        low_ref[:, at] = low
        terms = product(texts, [high, low], NN, 1) * inv
        for k, ref in enumerate((own_ref, first_ref, second_ref, across_ref)):
            ref[:, at] = terms[k * chunk : (k + 1) * chunk]


def text_kernel(me_ref, high_ref, low_ref, images_high_ref, images_low_ref, keep_ref, send_ref, all_ref):
    inv = all_ref.shape[0] ** (-0.5)
    images = [images_high_ref[...], images_low_ref[...]]
    total = product(images, [high_ref[...], low_ref[...]], NT, 1)
    all_ref[...] = total * inv
    n, step, _ = keep_ref.shape
    core, y = me_ref[0], me_ref[1]
    for k, there in enumerate(pairs(y, 1, n)):
        for other, ref in enumerate((keep_ref, send_ref)):
            ref[k] = all_ref[place(me_ref, there, core ^ other, step, all_ref.shape[0] // 4), :]


def sum_kernel(a_ref, b_ref, c_ref, after_ref, out_ref):
    del after_ref
    out_ref[...] = a_ref[...] + b_ref[...] + c_ref[...]


def gather(block, axis, n):
    return lax.all_to_all(jnp.broadcast_to(block[None], (n,) + block.shape), axis, 0, 0)


def after(x, *others):
    return pl.pallas_call(
        lambda *refs: None,
        out_shape=jax.ShapeDtypeStruct(x.shape, x.dtype),
        in_specs=[ANY] * (1 + len(others)),
        out_specs=ANY,
        input_output_aliases={0: 0},
        compiler_params=PARAMS,
        name="after",
    )(x, *others)


def sum_of(a, b, c, then):
    return pl.pallas_call(
        sum_kernel,
        out_shape=jax.ShapeDtypeStruct(a.shape, a.dtype),
        in_specs=[VMEM, VMEM, VMEM, ANY],
        compiler_params=PARAMS,
        name="sum",
    )(a, b, c, then)


def flip(n, bit):
    return [(i, i ^ bit) for i in range(n)]


def shifts(n):
    return [
        [(i, (i + 1) % n) for i in range(n)],
        [(i, (i - 1) % n) for i in range(n)],
        [(i, (i + 2 - 4 * (i % 2)) % n) for i in range(n)],
    ]


def neighbours(nx, nc):
    first, second = (1, 3), (3, 1)
    return [
        [(c * nx + x, c * nx + (x ^ apart[c])) for c in range(nc) for x in range(nx)]
        for apart in (first, second)
    ]


def body(image_embeddings, text_embeddings, negatives_mask):
    ny, nc, nx, nz = (lax.axis_size(a) for a in (Y, "core", "x", "z"))
    rows, own = image_embeddings.shape
    cols, own_text = text_embeddings.shape
    texts = text_embeddings.T
    far_half = lax.ppermute(texts, Y, flip(ny, ny // 2))
    images = gather(image_embeddings.T, "z", nz).reshape(nz * own, rows)
    texts = after(jnp.stack([texts, far_half]), images)
    images = after(images, far_half)
    to_first, to_second = neighbours(nx, nc)
    first = lax.ppermute(images, ("core", "x"), to_first)
    second = lax.ppermute(images, ("core", "x"), to_second)
    across = lax.ppermute(first, ("core", "x"), to_second)
    images = (images, first, second, across)
    near = gather(texts, "y_near", ny // 2).reshape(ny, own_text, cols)
    far = lax.ppermute(near + 0.0 * across[0, 0], "core", flip(nc, 1))
    width = nx * nz * own
    row_start = lax.axis_index(ROW) * rows
    col_start = lax.axis_index(COL) * cols
    row_blocks, col_blocks = rows // BLK, cols // BLK
    first_row, first_col = row_start // BLK, col_start // BLK
    window = lax.dynamic_slice(negatives_mask, (first_row, first_col), (row_blocks, col_blocks))
    row_ids = first_row + jnp.arange(row_blocks, dtype=jnp.int32)
    col_ids = first_col + jnp.arange(col_blocks, dtype=jnp.int32)
    allow = ((window > 0) | (row_ids[:, None] == col_ids[None, :])).astype(jnp.int32)
    f32, bf16 = jnp.float32, jnp.bfloat16
    passes = 2 * rows * cols * width
    me = [lax.axis_index("core"), lax.axis_index(Y), row_start, col_start, lax.axis_index("x")]
    me = jnp.stack(me).astype(jnp.int32)
    logits, row_parts, col_parts, images_high, images_low, texts_high, texts_low = pl.pallas_call(
        logits_kernel,
        out_shape=(
            jax.ShapeDtypeStruct((cols, rows), f32),
            jax.ShapeDtypeStruct((nx * nz, rows // LANES, LANES), f32),
            jax.ShapeDtypeStruct((ny * nc, rows // LANES, LANES), f32),
            jax.ShapeDtypeStruct((width, rows), bf16),
            jax.ShapeDtypeStruct((width, rows), bf16),
            jax.ShapeDtypeStruct((width, cols), bf16),
            jax.ShapeDtypeStruct((width, cols), bf16),
        ),
        in_specs=[SMEM, SMEM] + [VMEM] * 6,
        out_specs=(VMEM,) * 7,
        scratch_shapes=[pltpu.VMEM((width, cols), f32)],
        compiler_params=PARAMS,
        cost_estimate=pl.CostEstimate(flops=6 * passes, bytes_accessed=5 << 20, transcendentals=0),
        name="logits",
    )(me, allow, *images, near, far)
    row_parts = lax.all_to_all(row_parts, COL, 0, 0)
    col_parts = lax.all_to_all(after(col_parts, row_parts), ROW, 0, 0)
    own_terms, first, second, across, high, low = pl.pallas_call(
        image_kernel,
        out_shape=(jax.ShapeDtypeStruct((nz * own, rows), f32),) * 4
        + (jax.ShapeDtypeStruct((cols, rows), bf16),) * 2,
        in_specs=[SMEM] + [VMEM] * 5,
        out_specs=(VMEM,) * 6,
        compiler_params=PARAMS,
        cost_estimate=pl.CostEstimate(flops=3 * passes, bytes_accessed=5 << 20, transcendentals=0),
        name="image_terms",
    )(me, logits, row_parts, col_parts, texts_high, texts_low)
    half = jax.ShapeDtypeStruct((ny, own_text, cols), f32)
    keep, send = pl.pallas_call(
        text_kernel,
        out_shape=(half, half),
        in_specs=[SMEM] + [VMEM] * 4,
        out_specs=(VMEM, VMEM),
        scratch_shapes=[pltpu.VMEM((width, cols), f32)],
        compiler_params=PARAMS,
        cost_estimate=pl.CostEstimate(flops=3 * passes, bytes_accessed=5 << 20, transcendentals=0),
        name="text_terms",
    )(me, high, low, images_high, images_low)
    across = lax.ppermute(across, ("core", "x"), to_second)
    second = lax.ppermute(second, ("core", "x"), to_second)
    first = lax.ppermute(first + across, ("core", "x"), to_first)
    grad_text = keep + lax.ppermute(send, "core", flip(nc, 1))
    grad_text = grad_text.reshape(4, 2, own_text, cols)
    moved = [lax.ppermute(grad_text[k + 1], Y, perm) for k, perm in enumerate(shifts(ny))]
    parts = sum_of(own_terms, first, second, moved[0] + moved[1])
    grad_text = sum(moved, grad_text[0])
    grad_text = grad_text[0] + lax.ppermute(grad_text[1], Y, flip(ny, ny // 2))
    grad_image = jnp.sum(lax.all_to_all(parts.reshape(nz, own, rows), "z", 0, 0), axis=0)
    return (grad_image.T, grad_text.T)


def solution(mesh):
    rows, cols = mesh.devices.shape
    fine = Mesh(mesh.devices.reshape(2, rows // 4, 2, 4, cols // 4), ROW + COL)
    return jax.shard_map(
        body,
        mesh=fine,
        in_specs=(P(ROW, COL), P(COL, ROW), P()),
        out_specs=(P(ROW, COL), P(COL, ROW)),
        check_vma=False,
    )
```

```python
import functools

import jax
import jax.numpy as jnp
from jax import lax
from jax.experimental import pallas as pl
from jax.experimental.pallas import tpu as pltpu
from jax.sharding import Mesh
from jax.sharding import PartitionSpec as P

BLK = 256
LANES = 128
NEG = -1e30
Y = ("y_far", "y_near")
ROW = Y + ("core",)
COL = ("x", "z")
VMEM = pl.BlockSpec(memory_space=pltpu.VMEM)
HBM = pl.BlockSpec(memory_space=pltpu.HBM)
SMEM = pl.BlockSpec(memory_space=pltpu.SMEM)
ANY = pl.BlockSpec(memory_space=pl.ANY)
PARAMS = pltpu.CompilerParams(vmem_limit_bytes=24 * 2**20)
NN = (((1,), (0,)), ((), ()))
NT = (((1,), (1,)), ((), ()))


def split(x, terms):
    out = []
    for _ in range(terms):
        out.append(x.astype(jnp.bfloat16))
        x = x - out[-1].astype(jnp.float32)
    return out


def product(a, b, dims, order):
    total = None
    for both in range(order, -1, -1):
        for i in range(both + 1):
            if i < len(a) and both - i < len(b):
                p = lax.dot_general(a[i], b[both - i], dims, preferred_element_type=jnp.float32)
                total = p if total is None else total + p
    return total


def place(me_ref, there, core, step, chunk):
    shard = there * 2 + core
    per = chunk // step
    apart = (shard // per) ^ me_ref[4]
    first = 1 + me_ref[0]
    order = jnp.where(apart == 0, 0, jnp.where(apart == 1, first, jnp.where(apart == 3, 3 - first, 3)))
    return pl.ds(pl.multiple_of(order * chunk + (shard & (per - 1)) * step, step), step)


def arrange(me_ref, near_ref, far_ref, texts_ref):
    n, step, _ = near_ref.shape
    core, y = me_ref[0], me_ref[1]
    for k in range(n):
        there = (((y // (n // 2)) ^ (k % 2)) * (n // 2)) + k // 2
        for other, ref in enumerate((near_ref, far_ref)):
            texts_ref[place(me_ref, there, core ^ other, step, texts_ref.shape[0] // 4), :] = ref[k]


def pairs(y, way, n):
    two = y + way * (2 - 4 * (y & 1))
    return [(at + half) & (n - 1) for at in (y, y + way, y - way, two) for half in (0, n // 2)]


def logits_kernel(
    me_ref, allow_ref, own_ref, first_ref, second_ref, across_ref, near_ref, far_ref,
    logits_ref, row_ref, col_ref, images_high_ref, images_low_ref, texts_high_ref, texts_low_ref, texts_ref,
):
    rows = own_ref.shape[1]
    width, cols = texts_ref.shape
    inv = width ** (-0.5)
    arrange(me_ref, near_ref, far_ref, texts_ref)
    texts_high_ref[...], texts_low_ref[...] = split(texts_ref[...], 2)
    texts = split(texts_ref[...].T, 3)
    for i in range(rows // BLK):
        at = pl.ds(i * BLK, BLK)
        images = jnp.concatenate([ref[:, at] for ref in (own_ref, first_ref, second_ref, across_ref)])
        images = split(images, 3)
        images_high_ref[:, at] = images[0]
        images_low_ref[:, at] = images[1]
        part = product(texts, images, NN, 2) * inv
        for j in range(cols // BLK):
            block = jnp.where(allow_ref[i, j] > 0, part[j * BLK : (j + 1) * BLK], NEG)
            logits_ref[pl.ds(j * BLK, BLK), at] = block
        part = logits_ref[:, at]
        top = jnp.max(part, axis=0, keepdims=True)
        lse = top + jnp.log(jnp.sum(jnp.exp(part - top), axis=0, keepdims=True))
        put(row_ref, lse, i * BLK // LANES)
    for j in range(cols // BLK):
        part = logits_ref[pl.ds(j * BLK, BLK), :]
        top = jnp.max(part, axis=1, keepdims=True)
        lse = top + jnp.log(jnp.sum(jnp.exp(part - top), axis=1, keepdims=True))
        lse = jnp.broadcast_to(lse, (BLK, LANES)).T[:1]
        for first in range(j * BLK // LANES, col_ref.shape[1], cols // LANES):
            put(col_ref, lse, first)


def put(ref, values, first):
    for k in range(values.shape[1] // LANES):
        row = values[:, k * LANES : (k + 1) * LANES]
        ref[:, pl.ds(first + k, 1), :] = jnp.broadcast_to(row[None], (ref.shape[0], 1, LANES))


def lse_of(parts):
    top = jnp.max(parts, axis=0)
    return top + jnp.log(jnp.sum(jnp.exp(parts - top[None]), axis=0))


def gradient(me_ref, logits_ref, row_ref, col_ref):
    cols, rows = logits_ref.shape
    row_lse = lse_of(row_ref[...])
    col_lse = lse_of(col_ref[...])
    col_lse = jnp.concatenate(
        [jnp.broadcast_to(col_lse[k : k + 1], (LANES, LANES)).T[:, :1] for k in range(cols // LANES)]
    )
    ahead = me_ref[2] - me_ref[3]
    for i in range(rows // BLK):
        part = logits_ref[:, pl.ds(i * BLK, BLK)]
        first = i * BLK // LANES
        row = jnp.concatenate([row_lse[first + k : first + k + 1] for k in range(BLK // LANES)], axis=1)
        grad = 0.5 * (jnp.exp(part - row) + jnp.exp(part - col_lse))
        text_at = lax.broadcasted_iota(jnp.int32, grad.shape, 0)
        image_at = lax.broadcasted_iota(jnp.int32, grad.shape, 1) + (i * BLK + ahead)
        yield pl.ds(i * BLK, BLK), jnp.where(text_at == image_at, grad - 1.0, grad)


def image_kernel(
    me_ref, logits_ref, row_ref, col_ref, texts_high_ref, texts_low_ref,
    own_ref, first_ref, second_ref, across_ref, high_ref, low_ref,
):
    inv = texts_high_ref.shape[0] ** (-0.5)
    texts = [texts_high_ref[...], texts_low_ref[...]]
    chunk = own_ref.shape[0]
    for at, grad in gradient(me_ref, logits_ref, row_ref, col_ref):
        high, low = split(grad, 2)
        high_ref[:, at] = high
        low_ref[:, at] = low
        terms = product(texts, [high, low], NN, 1) * inv
        for k, ref in enumerate((own_ref, first_ref, second_ref, across_ref)):
            ref[:, at] = terms[k * chunk : (k + 1) * chunk]


def text_kernel(me_ref, high_ref, low_ref, images_high_ref, images_low_ref, keep_ref, send_ref, all_ref):
    inv = all_ref.shape[0] ** (-0.5)
    images = [images_high_ref[...], images_low_ref[...]]
    total = product(images, [high_ref[...], low_ref[...]], NT, 1)
    all_ref[...] = total * inv
    n, step, _ = keep_ref.shape
    core, y = me_ref[0], me_ref[1]
    for k, there in enumerate(pairs(y, 1, n)):
        for other, ref in enumerate((keep_ref, send_ref)):
            ref[k] = all_ref[place(me_ref, there, core ^ other, step, all_ref.shape[0] // 4), :]


def sum_kernel(a_ref, b_ref, c_ref, after_ref, out_ref):
    del after_ref
    out_ref[...] = a_ref[...] + b_ref[...] + c_ref[...]


def gather(block, axis, n):
    return lax.all_to_all(jnp.broadcast_to(block[None], (n,) + block.shape), axis, 0, 0)


def after(x, *others):
    return pl.pallas_call(
        lambda *refs: None,
        out_shape=jax.ShapeDtypeStruct(x.shape, x.dtype),
        in_specs=[ANY] * (1 + len(others)),
        out_specs=ANY,
        input_output_aliases={0: 0},
        compiler_params=PARAMS,
        name="after",
    )(x, *others)


def copy_kernel(*refs):
    refs[-1][...] = refs[0][...]


def copy_after(x, *others):
    return pl.pallas_call(
        copy_kernel,
        out_shape=jax.ShapeDtypeStruct(x.shape, x.dtype),
        in_specs=[VMEM] + [ANY] * len(others),
        out_specs=VMEM,
        compiler_params=PARAMS,
        name="copy",
    )(x, *others)


def sum_of(a, b, c, then):
    return pl.pallas_call(
        sum_kernel,
        out_shape=jax.ShapeDtypeStruct(a.shape, a.dtype),
        in_specs=[VMEM, VMEM, VMEM, ANY],
        compiler_params=PARAMS,
        name="sum",
    )(a, b, c, then)


def flip(n, bit):
    return [(i, i ^ bit) for i in range(n)]


def shifts(n):
    return [
        [(i, (i + 1) % n) for i in range(n)],
        [(i, (i - 1) % n) for i in range(n)],
        [(i, (i + 2 - 4 * (i % 2)) % n) for i in range(n)],
    ]


def neighbours(nx, nc):
    first, second = (1, 3), (3, 1)
    return [
        [(c * nx + x, c * nx + (x ^ apart[c])) for c in range(nc) for x in range(nx)]
        for apart in (first, second)
    ]


def body(image_embeddings, text_embeddings, negatives_mask):
    ny, nc, nx, nz = (lax.axis_size(a) for a in (Y, "core", "x", "z"))
    rows, own = image_embeddings.shape
    cols, own_text = text_embeddings.shape
    texts = text_embeddings.T
    far_half = lax.ppermute(texts, Y, flip(ny, ny // 2))
    images = gather(image_embeddings.T, "z", nz).reshape(nz * own, rows)
    texts = after(jnp.stack([texts, far_half]), images)
    images = after(images, far_half)
    to_first, to_second = neighbours(nx, nc)
    first = lax.ppermute(images, ("core", "x"), to_first)
    second = lax.ppermute(images, ("core", "x"), to_second)
    across = lax.ppermute(first, ("core", "x"), to_second)
    images = (images, first, second, across)
    near = gather(texts, "y_near", ny // 2).reshape(ny, own_text, cols)
    near = copy_after(near, across)
    far = lax.ppermute(near, "core", flip(nc, 1))
    width = nx * nz * own
    row_start = lax.axis_index(ROW) * rows
    col_start = lax.axis_index(COL) * cols
    row_blocks, col_blocks = rows // BLK, cols // BLK
    first_row, first_col = row_start // BLK, col_start // BLK
    window = lax.dynamic_slice(negatives_mask, (first_row, first_col), (row_blocks, col_blocks))
    row_ids = first_row + jnp.arange(row_blocks, dtype=jnp.int32)
    col_ids = first_col + jnp.arange(col_blocks, dtype=jnp.int32)
    allow = ((window > 0) | (row_ids[:, None] == col_ids[None, :])).astype(jnp.int32)
    f32, bf16 = jnp.float32, jnp.bfloat16
    passes = 2 * rows * cols * width
    me = [lax.axis_index("core"), lax.axis_index(Y), row_start, col_start, lax.axis_index("x")]
    me = jnp.stack(me).astype(jnp.int32)
    logits, row_parts, col_parts, images_high, images_low, texts_high, texts_low = pl.pallas_call(
        logits_kernel,
        out_shape=(
            jax.ShapeDtypeStruct((cols, rows), f32),
            jax.ShapeDtypeStruct((nx * nz, rows // LANES, LANES), f32),
            jax.ShapeDtypeStruct((ny * nc, rows // LANES, LANES), f32),
            jax.ShapeDtypeStruct((width, rows), bf16),
            jax.ShapeDtypeStruct((width, rows), bf16),
            jax.ShapeDtypeStruct((width, cols), bf16),
            jax.ShapeDtypeStruct((width, cols), bf16),
        ),
        in_specs=[SMEM, SMEM] + [VMEM] * 6,
        out_specs=(VMEM,) * 7,
        scratch_shapes=[pltpu.VMEM((width, cols), f32)],
        compiler_params=PARAMS,
        cost_estimate=pl.CostEstimate(flops=6 * passes, bytes_accessed=5 << 20, transcendentals=0),
        name="logits",
    )(me, allow, *images, near, far)
    row_parts = lax.all_to_all(row_parts, COL, 0, 0)
    col_parts = lax.all_to_all(after(col_parts, row_parts), ROW, 0, 0)
    own_terms, first, second, across, high, low = pl.pallas_call(
        image_kernel,
        out_shape=(jax.ShapeDtypeStruct((nz * own, rows), f32),) * 4
        + (jax.ShapeDtypeStruct((cols, rows), bf16),) * 2,
        in_specs=[SMEM] + [VMEM] * 5,
        out_specs=(VMEM,) * 6,
        compiler_params=PARAMS,
        cost_estimate=pl.CostEstimate(flops=3 * passes, bytes_accessed=5 << 20, transcendentals=0),
        name="image_terms",
    )(me, logits, row_parts, col_parts, texts_high, texts_low)
    half = jax.ShapeDtypeStruct((ny, own_text, cols), f32)
    keep, send = pl.pallas_call(
        text_kernel,
        out_shape=(half, half),
        in_specs=[SMEM] + [VMEM] * 4,
        out_specs=(VMEM, VMEM),
        scratch_shapes=[pltpu.VMEM((width, cols), f32)],
        compiler_params=PARAMS,
        cost_estimate=pl.CostEstimate(flops=3 * passes, bytes_accessed=5 << 20, transcendentals=0),
        name="text_terms",
    )(me, high, low, images_high, images_low)
    across = lax.ppermute(across, ("core", "x"), to_second)
    second = lax.ppermute(second, ("core", "x"), to_second)
    first = lax.ppermute(first + across, ("core", "x"), to_first)
    grad_text = keep + lax.ppermute(send, "core", flip(nc, 1))
    grad_text = grad_text.reshape(4, 2, own_text, cols)
    moved = [lax.ppermute(grad_text[k + 1], Y, perm) for k, perm in enumerate(shifts(ny))]
    parts = sum_of(own_terms, first, second, moved[0] + moved[1])
    grad_text = sum(moved, grad_text[0])
    grad_text = grad_text[0] + lax.ppermute(grad_text[1], Y, flip(ny, ny // 2))
    grad_image = jnp.sum(lax.all_to_all(parts.reshape(nz, own, rows), "z", 0, 0), axis=0)
    return (grad_image.T, grad_text.T)


def solution(mesh):
    rows, cols = mesh.devices.shape
    fine = Mesh(mesh.devices.reshape(2, rows // 4, 2, 4, cols // 4), ROW + COL)
    return jax.shard_map(
        body,
        mesh=fine,
        in_specs=(P(ROW, COL), P(COL, ROW), P()),
        out_specs=(P(ROW, COL), P(COL, ROW)),
        check_vma=False,
    )
```
